512 devices in a mesh: space: 64 (over y_lo, z, x), tm: 8 (over y_hi, core).
Axes of the slice: x: 4, y: 8 (y_hi: 4, y_lo: 2; y = y_hi * 2 + y_lo), z: 8, core: 2. Of those that a mesh axis runs over, the one named last changes fastest.
Arguments:
- strain: bfloat16 [3, 2112, 65536], P(None, 'tm', 'space'), may hold values from -400 to 400
- block_starts: int32 [64], replicated, may hold values from 0 to 2023, as said below
- bin_numbers: int32 [16], replicated, may hold values from 1 to 31
Outputs:
- upper_factor: float32 [16, 128, 128], replicated
- mode_basis: bfloat16 [16, 128, 3, 65536], P(None, None, None, ('space', 'tm'))
The draws below stay inside these ranges and needn't reach their ends.
Inputs may be any that keep to these rules, and one draw needn't show every extreme that they name: `block_starts`: block b starts at b * 32 plus a shift of 0 to 7; the first block's shift is 0 and the last block's is 7.
All inputs are finite; a program needn't handle non-finite values.
Results may differ from the reference program's by a relative error of at most 0.009.
Values may be sent and summed in bfloat16 or wider, within the bound.
A program may use at most 64 MiB of HBM per device.

```python
import math
import jax
import jax.numpy as jnp
from jax import lax

NFFT = 64
NB = 64
NF = 16
JITTER = 8
PTS = 128
NT = 2112
POINTS = 65536


def draw_block_starts(key, part):
    key = jax.random.fold_in(key, 11)
    shifts = jax.random.randint(key, (NB,), 0, JITTER)
    shifts = shifts.at[0].set(0).at[NB - 1].set(JITTER - 1)
    return (jnp.arange(NB, dtype=jnp.int32) * (NFFT // 2) + shifts).astype(jnp.int32)


def draw_strain(key, part):
    key = jax.random.fold_in(key, 23)
    keys_all = jax.random.split(key, 6)
    block_total = POINTS // PTS
    place = jnp.arange(POINTS, dtype=jnp.float32)
    profile = jnp.sqrt(1.0 + 2.0 * place / POINTS)
    patches = jnp.exp(jax.random.uniform(keys_all[0], (block_total,), jnp.float32, math.log(0.3), math.log(3.0)))
    heavy_block = jax.random.randint(keys_all[5], (), 0, block_total)
    heavy_gain = math.sqrt(0.5 * block_total)
    patches = jnp.where(jnp.arange(block_total) == heavy_block, jnp.float32(heavy_gain), patches)
    patch_gain = jnp.repeat(patches, PTS)
    point_gain = jnp.exp(jax.random.uniform(keys_all[1], (POINTS,), jnp.float32, math.log(0.5), math.log(2.0)))
    mixing = jax.random.truncated_normal(keys_all[2], -3.0, 3.0, (POINTS,), jnp.float32)
    noise = jax.random.truncated_normal(keys_all[3], -4.0, 4.0, (3, NT, POINTS), jnp.float32)
    common = 0.3 * jax.random.truncated_normal(keys_all[4], -4.0, 4.0, (3, NT, 1), jnp.float32)
    amplitude = profile * patch_gain * point_gain
    return (amplitude * (noise + common * mixing)).astype(jnp.bfloat16)


def set_ends(drawn, own_key, smallest, high):
    spot = [jax.random.randint(jax.random.fold_in(own_key, axis), (), 0, length) for axis, length in enumerate(drawn.shape)]
    main_axis = drawn.shape.index(max(drawn.shape))
    next_to = spot[:main_axis] + [(spot[main_axis] + 1) % drawn.shape[main_axis]] + spot[main_axis + 1:]
    return drawn.at[tuple(spot)].set(smallest).at[tuple(next_to)].set(high)


def setup_inputs(seed: int = 0) -> dict:
    key_of = jax.random.split(jax.random.key(seed), 4)
    strain = draw_strain(jax.random.fold_in(key_of[3], 71), 0)
    block_starts = draw_block_starts(jax.random.fold_in(key_of[3], 71), 0)
    bin_numbers = set_ends(jax.random.randint(key_of[2], (NF,), 1, NFFT // 2), jax.random.fold_in(key_of[2], 1), 1, (NFFT // 2) - 1).astype(jnp.int32)
    return dict(strain=strain, block_starts=block_starts, bin_numbers=bin_numbers)


def window_table(bin_numbers):
    sample_steps = jnp.arange(NFFT, dtype=jnp.int32)
    hann_taper = (1.0 - jnp.cos(2.0 * math.pi * sample_steps.astype(jnp.float32) / NFFT)) / math.sqrt(1.5 * NFFT)
    phase_turns = (bin_numbers[:, None] * sample_steps[None, :] % NFFT).astype(jnp.float32)
    angle_rows = 2.0 * math.pi * phase_turns / NFFT
    stacked = jnp.stack([hann_taper * jnp.cos(angle_rows), -hann_taper * jnp.sin(angle_rows)], axis=1)
    return stacked.reshape(2 * bin_numbers.shape[0], NFFT).astype(jnp.bfloat16)

def spectra(history, block_starts, window_rows):
    positions = block_starts[:, None] + jnp.arange(NFFT, dtype=jnp.int32)[None, :]
    segments = jnp.take(history, positions, axis=1)
    return jnp.einsum('kt,cbtp->kbcp', window_rows.astype(jnp.float32), segments.astype(jnp.float32), precision=lax.Precision.HIGHEST)

def reference(strain, block_starts, bin_numbers):
    window_rows = window_table(bin_numbers)
    block_count = POINTS // PTS

    def columns_of(block_index):
        history = lax.dynamic_slice_in_dim(strain, block_index * PTS, PTS, 2)
        return spectra(history, block_starts, window_rows).reshape(NF, 2 * NB, 3 * PTS)

    def accumulate(running, block_index):
        columns_now = columns_of(block_index)
        product = jnp.einsum('fjr,fkr->fjk', columns_now, columns_now, precision=lax.Precision.HIGHEST)
        return (running + product, None)
    start_sum = jnp.zeros((NF, 2 * NB, 2 * NB), jnp.float32)
    running, _ = lax.scan(accumulate, start_sum, jnp.arange(block_count, dtype=jnp.int32))
    gram_matrix = running / (3.0 * POINTS)
    lower_factor = jnp.linalg.cholesky(gram_matrix)

    def solve_block(block_index):
        columns_now = columns_of(block_index)
        solved = lax.linalg.triangular_solve(lower_factor, columns_now, left_side=True, lower=True)
        return solved.astype(jnp.bfloat16).reshape(NF, 2 * NB, 3, PTS)
    solved_blocks = lax.map(solve_block, jnp.arange(block_count, dtype=jnp.int32))
    mode_basis = jnp.moveaxis(solved_blocks, 0, 3).reshape(NF, 2 * NB, 3, POINTS)
    return (jnp.swapaxes(lower_factor, 1, 2), mode_basis)
```

```python
import functools
import math

import jax
import jax.numpy as jnp
from jax import lax
from jax.experimental import pallas as pl
from jax.experimental.pallas import tpu as pltpu
from jax.sharding import PartitionSpec as P

NFFT = 64
HOP = 32
MESH = pl.DeviceIdType.MESH
F32 = jnp.float32
BF16 = jnp.bfloat16

NX, NZ, NY, NT = 4, 8, 8, 8


def window_table(bin_numbers):
    sample_steps = jnp.arange(NFFT, dtype=jnp.int32)
    hann_taper = (
        1.0 - jnp.cos(2.0 * math.pi * sample_steps.astype(F32) / NFFT)
    ) / math.sqrt(1.5 * NFFT)
    phase_turns = (bin_numbers[:, None] * sample_steps[None, :] % NFFT).astype(F32)
    angle_rows = 2.0 * math.pi * phase_turns / NFFT
    stacked = jnp.stack(
        [hann_taper * jnp.cos(angle_rows), -hann_taper * jnp.sin(angle_rows)], axis=1
    )
    return stacked.reshape(2 * bin_numbers.shape[0], NFFT).astype(BF16)


def iota(shape, dim):
    return lax.broadcasted_iota(jnp.int32, shape, dim)


def dot(a, b):
    return jnp.dot(a, b, preferred_element_type=F32)


def dot_t(a, b):
    return lax.dot_general(a, b, (((1,), (1,)), ((), ())), preferred_element_type=F32)


def place():
    s, t = lax.axis_index("space"), lax.axis_index("tm")
    x = lax.rem(s, NX)
    z = lax.rem(lax.div(s, NX), NZ)
    ylo = lax.div(s, NX * NZ)
    core = lax.rem(t, 2)
    yhi = lax.div(t, 2)
    return s, t, x, z, ylo, core, yhi


def space_of(x, z, ylo):
    return (ylo * NZ + z) * NX + x


def remote(src, dst, send, recv, device):
    return pltpu.make_async_remote_copy(
        src_ref=src, dst_ref=dst, send_sem=send, recv_sem=recv,
        device_id=device, device_id_type=MESH,
    )


FAR_T = (4, 5, 3, 2, 6, 7, 1)
FAR_8 = (4, 3, 5, 2, 6, 1, 7)
FAR_4 = (2, 1, 3)


def build_windows(starts, window, amat, mmat):
    tile = (lax.rem(iota((NFFT, 512), 1), NFFT) == iota((NFFT, 512), 0)).astype(BF16)
    tiled = dot(window[...], tile).astype(BF16)
    spread = (lax.div(iota((256, 32), 0), 8) == iota((256, 32), 1)).astype(BF16)
    full = dot(spread, tiled)
    same = lax.rem(iota((256, 512), 0), 8) == lax.div(iota((256, 512), 1), NFFT)
    amat[...] = jnp.where(same, full, 0.0).astype(BF16)
    slot = iota((NFFT, 384), 1)
    when = jnp.where(slot < 264, slot, jnp.where(slot < 304, slot - 8, slot - 376))
    real = (slot < 264) | ((slot >= 272) & (slot < 304)) | ((slot >= 304) & (slot < 376))
    when = jnp.where(real, when, -100000) - iota((NFFT, 384), 0)
    for g in range(8):
        parts = []
        for b in range(8):
            begin = starts[8 * g + b] - 264 * g
            parts.append(jnp.where(when == begin, 1.0, 0.0).astype(BF16))
        pick = jnp.concatenate(parts, axis=0)
        mmat[g] = dot(amat[...], pick).astype(BF16)


def first_kernel(
    strain, starts, window, zout, gout,
    came, slab, amat, mmat, spec, zbuf, gram, packed, rc, sum4, rx, pz, rz, piece, ry, fin, gz,
    a_send, a_recv, own_sem, c_send, c_recv, x_send, x_recv, z_send, z_recv,
    y_send, y_recv, w_send, w_recv, out_sem,
):
    s, t, x, z, ylo, core, yhi = place()
    yy = yhi * 2 + ylo
    tm_peers = [(s, lax.rem(t + o, NT)) for o in range(1, NT)]
    x_peers = {o: (space_of(lax.rem(x + o, NX), z, ylo), t) for o in FAR_4}
    z_peers = {o: (space_of(x, lax.rem(z + o, NZ), ylo), t) for o in FAR_8}

    def y_peer(o):
        other = lax.rem(yy + o, NY)
        return (space_of(x, z, lax.rem(other, 2)), lax.div(other, 2) * 2 + core)

    y_peers = {o: y_peer(o) for o in FAR_8}
    mate = (s, t + 1 - 2 * core)

    barrier = pltpu.get_barrier_semaphore()
    odd = {o: y_peers[o] for o in (1, 3, 5, 7)}
    greeted = tm_peers + list(x_peers.values()) + list(z_peers.values()) + list(odd.values())
    for peer in greeted:
        pl.semaphore_signal(barrier, inc=1, device_id=peer, device_id_type=MESH)
    pl.semaphore_wait(barrier, len(greeted))

    sends = []
    for c in range(3):
        for o in FAR_T:
            to = lax.rem(t + o, NT)
            copy = remote(
                strain.at[c, :, pl.ds(pl.multiple_of(to * 128, 128), 128)],
                came.at[t, c], a_send.at[o, c], a_recv.at[o, c], (s, to),
            )
            copy.start()
            sends.append(copy)
    own = pltpu.make_async_copy(
        strain.at[:, :, pl.ds(pl.multiple_of(t * 128, 128), 128)], came.at[t], own_sem
    )
    own.start()

    build_windows(starts, window, amat, mmat)
    slab[...] = jnp.zeros_like(slab)
    own.wait()

    for c in range(3):
        for o in FAR_T:
            source = lax.rem(t + NT - o, NT)
            remote(
                came.at[source, c], came.at[source, c], a_send.at[o, c], a_recv.at[o, c], (s, source)
            ).wait_recv()
        for g in range(8):
            slab[g, 0:264, :] = came[g, c, :, :]
            if g < 7:
                slab[g, 272:304, :] = came[g + 1, c, 0:32, :]
            if g > 0:
                slab[g, 304:376, :] = came[g - 1, c, 192:264, :]
        for g in range(8):
            found = dot(mmat[g], slab[g])
            spec[:, 8 * g : 8 * g + 8, :] = found.reshape(32, 8, 128)

        def one(f, carry, c=c):
            rows = spec[pl.ds(2 * f, 2)].reshape(128, 128)
            high = rows.astype(BF16)
            low = (rows - high.astype(F32)).astype(BF16)
            both = jnp.concatenate([high, low], axis=0)
            zbuf[f, :, 128 * c : 128 * c + 128] = both
            quad = dot_t(both, both)
            new = (quad[:128, :128] + quad[128:, 128:]) + (quad[:128, 128:] + quad[128:, :128])
            if c == 0:
                gram[f] = new
            else:
                gram[f] = gram[f] + new
            return carry

        lax.fori_loop(0, 16, one, 0)
    save = pltpu.make_async_copy(zbuf, zout, out_sem)
    save.start()

    row, col = iota((128, 128), 0), iota((128, 128), 1)
    for q in range(8):
        first, second = gram[2 * q], gram[2 * q + 1]
        packed[q, 0:128, :] = jnp.where(row > col, first, second)
        diag = jnp.sum(jnp.where(row == col, first, 0.0), axis=0, keepdims=True)
        packed[q, 128:136, :] = jnp.broadcast_to(diag, (8, 128))

    for o in FAR_4 + (0,):
        xo = lax.rem(x + o, NX)
        copy = remote(packed.at[(1 - core) * 4 + xo], rc.at[xo], c_send.at[o], c_recv.at[o], mate)
        copy.start()
        sends.append(copy)
    for o in FAR_4:
        xo = lax.rem(x + o, NX)
        remote(packed.at[xo], rc.at[xo], c_send.at[o], c_recv.at[o], mate).wait_recv()
        sum4[xo] = packed[core * 4 + xo] + rc[xo]
        copy = remote(sum4.at[xo], rx.at[x], x_send.at[o], x_recv.at[o], x_peers[o])
        copy.start()
        sends.append(copy)
    remote(packed.at[x], rc.at[x], c_send.at[0], c_recv.at[0], mate).wait_recv()
    rx[x] = packed[core * 4 + x] + rc[x]
    for o in FAR_4:
        source = lax.rem(x + NX - o, NX)
        remote(sum4.at[source], rx.at[source], x_send.at[o], x_recv.at[o], x_peers[o]).wait_recv()
    mine = (rx[0] + rx[1]) + (rx[2] + rx[3])

    for i in range(NZ):
        pz[i, 0:16, :] = mine[16 * i : 16 * i + 16]
        pz[i, 16:24, :] = mine[128:136]
    for o in FAR_8:
        zo = lax.rem(z + o, NZ)
        copy = remote(pz.at[zo], rz.at[z], z_send.at[o], z_recv.at[o], z_peers[o])
        copy.start()
        sends.append(copy)
    rz[z] = pz[z]
    for o in FAR_8:
        source = lax.rem(z + NZ - o, NZ)
        remote(pz.at[source], rz.at[source], z_send.at[o], z_recv.at[o], z_peers[o]).wait_recv()
    piece[...] = ((rz[0] + rz[1]) + (rz[2] + rz[3])) + ((rz[4] + rz[5]) + (rz[6] + rz[7]))

    for o in FAR_8:
        copy = remote(piece, ry.at[yy], y_send.at[o], y_recv.at[o], y_peers[o])
        copy.start()
        sends.append(copy)
    ry[yy] = piece[...]
    for o in FAR_8:
        source = lax.rem(yy + NY - o, NY)
        remote(piece, ry.at[source], y_send.at[o], y_recv.at[o], y_peers[o]).wait_recv()
    fin[...] = ((ry[0] + ry[1]) + (ry[2] + ry[3])) + ((ry[4] + ry[5]) + (ry[6] + ry[7]))

    for o in FAR_8:
        copy = remote(fin, gz.at[z], w_send.at[o], w_recv.at[o], z_peers[o])
        copy.start()
        sends.append(copy)
    gz[z] = fin[...]
    for o in FAR_8:
        source = lax.rem(z + NZ - o, NZ)
        remote(fin, gz.at[source], w_send.at[o], w_recv.at[o], z_peers[o]).wait_recv()
    gout[...] = gz[...]

    for copy in sends:
        copy.wait_send()
    save.wait()


def factor_kernel(total_rows, g, out):
    lanes, subs = iota((8, 128), 1), iota((8, 128), 0)
    row, col = iota((128, 128), 0), iota((128, 128), 1)
    square = jnp.concatenate([g[i, 0:16, :] for i in range(NZ)], axis=0) * (1.0 / total_rows)
    spare = g[0, 16:17, :] * (1.0 / total_rows)
    turned = square.T
    first = jnp.where(row == col, spare, jnp.where(row > col, square, turned))
    second = jnp.where(row > col, turned, square)
    mats = [[m[8 * v : 8 * v + 8] for v in range(16)] for m in (first, second)]
    for j in range(128):
        v0, r = j // 8, j % 8
        here = lanes == j
        for m in mats:
            top = m[v0]
            column = jnp.broadcast_to(top[:, j : j + 1], (8, 128))
            pivot = jnp.broadcast_to(column[r : r + 1, :], (8, 128))
            root = lax.rsqrt(pivot)
            root = root * (1.5 - 0.5 * pivot * root * root)
            across = jnp.broadcast_to(top[r : r + 1, :], (8, 128))
            across = jnp.where(here, 1.0, across) * root
            scaled = across * root
            new = jnp.where(here, 0.0, top) - column * scaled
            m[v0] = jnp.where(subs > r, new, jnp.where(subs == r, across, top))
            for v in range(v0 + 1, 16):
                column = jnp.broadcast_to(m[v][:, j : j + 1], (8, 128))
                m[v] = jnp.where(here, 0.0, m[v]) - column * scaled
    for k in range(2):
        for v in range(16):
            out[k, 8 * v : 8 * v + 8, :] = mats[k][v]


def gather_kernel(mine, out, held, x_send, x_recv, c_send, c_recv):
    s, t, x, z, ylo, core, yhi = place()
    mate = (s, t + 1 - 2 * core)
    x_peers = {o: (space_of(lax.rem(x + o, NX), z, ylo), t) for o in FAR_4}
    barrier = pltpu.get_barrier_semaphore()
    for peer in list(x_peers.values()) + [mate]:
        pl.semaphore_signal(barrier, inc=1, device_id=peer, device_id_type=MESH)
    pl.semaphore_wait(barrier, 4)
    sends = []
    for o in FAR_4:
        copy = remote(mine, held.at[core * 4 + x], x_send.at[o], x_recv.at[o], x_peers[o])
        copy.start()
        sends.append(copy)
    copy = remote(mine, held.at[core * 4 + x], c_send.at[0], c_recv.at[0], mate)
    copy.start()
    sends.append(copy)
    held[core * 4 + x] = mine[...]
    for o in (1, 3, 2):
        slot = core * 4 + lax.rem(x + NX - o, NX)
        remote(mine, held.at[slot], x_send.at[o], x_recv.at[o], x_peers[o]).wait_recv()
        copy = remote(held.at[slot], held.at[slot], c_send.at[o], c_recv.at[o], mate)
        copy.start()
        sends.append(copy)
    for o in (0, 1, 3, 2):
        slot = (1 - core) * 4 + lax.rem(x + NX - o, NX)
        remote(mine, held.at[slot], c_send.at[o], c_recv.at[o], mate).wait_recv()
    out[...] = held[...]
    for copy in sends:
        copy.wait_send()


def apply_kernel(pk, zz, upper, basis):
    row, col = iota((128, 128), 0), iota((128, 128), 1)
    for k in range(2):
        both = pk[0, k]
        upper[k] = jnp.where(col > row, both, jnp.where(col == row, 1.0 / both, 0.0))
        inverse = jnp.where(col <= row, both, 0.0)
        high = inverse.astype(BF16)
        low = (inverse - high.astype(F32)).astype(BF16)
        twice = jnp.concatenate([high, high], axis=1)
        found = dot(twice, zz[k]) + dot(low, zz[k, 0:128, :])
        for c in range(3):
            basis[k, c] = found[:, 128 * c : 128 * c + 128].astype(BF16)


def shards(strain, block_starts, bin_numbers):
    window = window_table(bin_numbers)
    vmem = pl.BlockSpec(memory_space=pltpu.VMEM)
    hbm = pl.BlockSpec(memory_space=pl.ANY)
    dma = pltpu.SemaphoreType.DMA
    total_rows = 3.0 * 128 * lax.axis_size("space") * lax.axis_size("tm")
    zz, summed = pl.pallas_call(
        first_kernel,
        out_shape=(
            jax.ShapeDtypeStruct((16, 256, 384), BF16),
            jax.ShapeDtypeStruct((NZ, 24, 128), F32),
        ),
        in_specs=[hbm, pl.BlockSpec(memory_space=pltpu.SMEM), vmem],
        out_specs=(hbm, vmem),
        scratch_shapes=[
            pltpu.VMEM((NT, 3, 264, 128), BF16),
            pltpu.VMEM((8, 384, 128), BF16),
            pltpu.VMEM((256, 512), BF16),
            pltpu.VMEM((8, 256, 384), BF16),
            pltpu.VMEM((32, 64, 128), F32),
            pltpu.VMEM((16, 256, 384), BF16),
            pltpu.VMEM((16, 128, 128), F32),
            pltpu.VMEM((8, 136, 128), F32),
            pltpu.VMEM((4, 136, 128), F32),
            pltpu.VMEM((4, 136, 128), F32),
            pltpu.VMEM((4, 136, 128), F32),
            pltpu.VMEM((NZ, 24, 128), F32),
            pltpu.VMEM((NZ, 24, 128), F32),
            pltpu.VMEM((24, 128), F32),
            pltpu.VMEM((NY, 24, 128), F32),
            pltpu.VMEM((24, 128), F32),
            pltpu.VMEM((NZ, 24, 128), F32),
            dma((NT, 3)), dma((NT, 3)), dma,
            dma((4,)), dma((4,)), dma((4,)), dma((4,)),
            dma((8,)), dma((8,)), dma((8,)), dma((8,)), dma((8,)), dma((8,)), dma,
        ],
        compiler_params=pltpu.CompilerParams(
            collective_id=0, has_side_effects=True, vmem_limit_bytes=40 * 1024 * 1024
        ),
    )(strain, block_starts, window)
    factor = pl.pallas_call(
        functools.partial(factor_kernel, total_rows),
        out_shape=jax.ShapeDtypeStruct((2, 128, 128), F32),
        in_specs=[vmem],
        out_specs=vmem,
    )(summed)
    held = pl.pallas_call(
        gather_kernel,
        out_shape=jax.ShapeDtypeStruct((8, 2, 128, 128), F32),
        in_specs=[vmem],
        out_specs=vmem,
        scratch_shapes=[
            pltpu.VMEM((8, 2, 128, 128), F32),
            dma((4,)), dma((4,)), dma((4,)), dma((4,)),
        ],
        compiler_params=pltpu.CompilerParams(
            collective_id=1, has_side_effects=True, vmem_limit_bytes=16 * 1024 * 1024
        ),
    )(factor)
    upper, basis = pl.pallas_call(
        apply_kernel,
        grid=(8,),
        out_shape=(
            jax.ShapeDtypeStruct((16, 128, 128), F32),
            jax.ShapeDtypeStruct((16, 3, 128, 128), BF16),
        ),
        in_specs=[
            pl.BlockSpec((1, 2, 128, 128), lambda i: (i, 0, 0, 0)),
            pl.BlockSpec((2, 256, 384), lambda i: (i, 0, 0)),
        ],
        out_specs=(
            pl.BlockSpec((2, 128, 128), lambda i: (i, 0, 0)),
            pl.BlockSpec((2, 3, 128, 128), lambda i: (i, 0, 0, 0)),
        ),
    )(held, zz)
    return upper, jnp.transpose(basis, (0, 2, 1, 3))


def solution(mesh):
    placed = (P(None, "tm", "space"), P(), P())
    return jax.shard_map(
        shards,
        mesh=mesh,
        in_specs=placed,
        out_specs=(P(), P(None, None, None, ("space", "tm"))),
        check_vma=False,
    )
```

```python
import functools
import math

import jax
import jax.numpy as jnp
from jax import lax
from jax.experimental import pallas as pl
from jax.experimental.pallas import tpu as pltpu
from jax.sharding import PartitionSpec as P

NFFT = 64
HOP = 32
MESH = pl.DeviceIdType.MESH
F32 = jnp.float32
BF16 = jnp.bfloat16

NX, NZ, NY, NT = 4, 8, 8, 8


def iota(shape, dim):
    return lax.broadcasted_iota(jnp.int32, shape, dim)


def dot(a, b):
    return jnp.dot(a, b, preferred_element_type=F32)


def dot_t(a, b):
    return lax.dot_general(a, b, (((1,), (1,)), ((), ())), preferred_element_type=F32)


def place():
    s, t = lax.axis_index("space"), lax.axis_index("tm")
    x = lax.rem(s, NX)
    z = lax.rem(lax.div(s, NX), NZ)
    ylo = lax.div(s, NX * NZ)
    core = lax.rem(t, 2)
    yhi = lax.div(t, 2)
    return s, t, x, z, ylo, core, yhi


def space_of(x, z, ylo):
    return (ylo * NZ + z) * NX + x


def remote(src, dst, send, recv, device):
    return pltpu.make_async_remote_copy(
        src_ref=src, dst_ref=dst, send_sem=send, recv_sem=recv,
        device_id=device, device_id_type=MESH,
    )


FAR_T = ((2, 0), (2, 1), (1, 0), (1, 1), (3, 0), (3, 1), (0, 1))
FAR_8 = (4, 3, 5, 2, 6, 1, 7)
FAR_4 = (2, 1, 3)


def build_windows(starts, bins, amat, mmat):
    step = iota((32, NFFT), 1)
    freq = lax.div(iota((32, NFFT), 0), 2)
    turns = jnp.zeros((32, NFFT), jnp.int32)
    for f in range(16):
        turns = jnp.where(freq == f, bins[f], turns)
    angle = (2.0 * math.pi) * lax.rem(turns * step, NFFT).astype(F32) / NFFT
    taper = (1.0 - jnp.cos((2.0 * math.pi) * step.astype(F32) / NFFT)) / math.sqrt(1.5 * NFFT)
    real = lax.rem(iota((32, NFFT), 0), 2) == 0
    window = (taper * jnp.where(real, jnp.cos(angle), -jnp.sin(angle))).astype(BF16)
    tile = (lax.rem(iota((NFFT, 512), 1), NFFT) == iota((NFFT, 512), 0)).astype(BF16)
    tiled = dot(window, tile).astype(BF16)
    spread = (lax.div(iota((256, 32), 0), 8) == iota((256, 32), 1)).astype(BF16)
    full = dot(spread, tiled)
    same = lax.rem(iota((256, 512), 0), 8) == lax.div(iota((256, 512), 1), NFFT)
    amat[...] = jnp.where(same, full, 0.0).astype(BF16)
    slot = iota((NFFT, 384), 1)
    when = jnp.where(slot < 264, slot, jnp.where(slot < 304, slot - 8, slot - 376))
    known = (slot < 264) | ((slot >= 272) & (slot < 304)) | ((slot >= 304) & (slot < 376))
    when = jnp.where(known, when, -100000) - iota((NFFT, 384), 0)
    for g in range(8):
        parts = []
        for b in range(8):
            begin = starts[8 * g + b] - 264 * g
            parts.append(jnp.where(when == begin, 1.0, 0.0).astype(BF16))
        pick = jnp.concatenate(parts, axis=0)
        mmat[g] = dot(amat[...], pick).astype(BF16)


def first_kernel(
    total_rows,     strain, starts, bins, zout, out,
    came, slab, amat, mmat, spec, zbuf, gram, packed, rc, sum4, rx, pz, rz, piece, ry, fin, gz, held,
    a_send, a_recv, own_sem, c_send, c_recv, x_send, x_recv, z_send, z_recv,
    y_send, y_recv, w_send, w_recv, f_send, f_recv, m_send, m_recv, out_sem,
):
    s, t, x, z, ylo, core, yhi = place()
    yy = yhi * 2 + ylo
    def tm_peer(dy, dc):
        return lax.rem(yhi + dy, 4) * 2 + lax.rem(core + dc, 2)

    tm_peers = [(s, tm_peer(*o)) for o in FAR_T]
    x_peers = {o: (space_of(lax.rem(x + o, NX), z, ylo), t) for o in FAR_4}
    z_peers = {o: (space_of(lax.rem(x + 8 - o, NX), lax.rem(z + o, NZ), ylo), t) for o in FAR_8}
    line = {o: (space_of(x, lax.rem(z + o, NZ), ylo), t) for o in (1, 2, 6, 7)}
    own = lax.rem(x + z, NX)

    def y_peer(o):
        other = lax.rem(yy + o, NY)
        return (space_of(x, z, lax.rem(other, 2)), lax.div(other, 2) * 2 + core)

    y_peers = {o: y_peer(o) for o in FAR_8}
    mate = (s, t + 1 - 2 * core)

    barrier = pltpu.get_barrier_semaphore()
    odd = {o: y_peers[o] for o in (1, 3, 5, 7)}
    greeted = tm_peers + list(x_peers.values()) + list(z_peers.values()) + list(odd.values()) + list(line.values())
    for peer in greeted:
        pl.semaphore_signal(barrier, inc=1, device_id=peer, device_id_type=MESH)
    pl.semaphore_wait(barrier, len(greeted))

    sends = []
    for c in range(3):
        for o in FAR_T:
            to = tm_peer(*o)
            n = o[0] * 2 + o[1]
            copy = remote(
                strain.at[c, :, pl.ds(pl.multiple_of(to * 128, 128), 128)],
                came.at[t, c], a_send.at[n, c], a_recv.at[n, c], (s, to),
            )
            copy.start()
            sends.append(copy)
    stay = pltpu.make_async_copy(
        strain.at[:, :, pl.ds(pl.multiple_of(t * 128, 128), 128)], came.at[t], own_sem
    )
    stay.start()

    build_windows(starts, bins, amat, mmat)
    slab[...] = jnp.zeros_like(slab)
    stay.wait()

    for c in range(3):
        for o in FAR_T:
            source = tm_peer(4 - o[0], o[1])
            n = o[0] * 2 + o[1]
            remote(
                came.at[source, c], came.at[source, c], a_send.at[n, c], a_recv.at[n, c], (s, source)
            ).wait_recv()
        for g in range(8):
            slab[g, 0:264, :] = came[g, c, :, :]
            if g < 7:
                slab[g, 272:304, :] = came[g + 1, c, 0:32, :]
            if g > 0:
                slab[g, 304:376, :] = came[g - 1, c, 192:264, :]
        for g in range(8):
            found = dot(mmat[g], slab[g])
            spec[:, 8 * g : 8 * g + 8, :] = found.reshape(32, 8, 128)

        def one(f, carry, c=c):
            rows = spec[pl.ds(2 * f, 2)].reshape(128, 128)
            high = rows.astype(BF16)
            low = (rows - high.astype(F32)).astype(BF16)
            both = jnp.concatenate([high, low], axis=0)
            zbuf[f, :, 128 * c : 128 * c + 128] = both
            quad = dot_t(both, both)
            new = (quad[:128, :128] + quad[128:, 128:]) + (quad[:128, 128:] + quad[128:, :128])
            if c == 0:
                gram[f] = new
            else:
                gram[f] = gram[f] + new
            return carry

        lax.fori_loop(0, 16, one, 0)
    save = pltpu.make_async_copy(zbuf, zout, out_sem)
    save.start()

    row, col = iota((128, 128), 0), iota((128, 128), 1)
    for q in range(8):
        first, second = gram[2 * q], gram[2 * q + 1]
        packed[q, 0:128, :] = jnp.where(row > col, first, second)
        diag = jnp.sum(jnp.where(row == col, first, 0.0), axis=0, keepdims=True)
        packed[q, 128:136, :] = jnp.broadcast_to(diag, (8, 128))

    for o in FAR_4 + (0,):
        xo = lax.rem(x + o, NX)
        pair = lax.rem(xo + z, NX)
        copy = remote(packed.at[(1 - core) * 4 + pair], rc.at[xo], c_send.at[o], c_recv.at[o], mate)
        copy.start()
        sends.append(copy)
    for o in FAR_4:
        xo = lax.rem(x + o, NX)
        remote(packed.at[xo], rc.at[xo], c_send.at[o], c_recv.at[o], mate).wait_recv()
        sum4[xo] = packed[core * 4 + lax.rem(xo + z, NX)] + rc[xo]
        copy = remote(sum4.at[xo], rx.at[x], x_send.at[o], x_recv.at[o], x_peers[o])
        copy.start()
        sends.append(copy)
    remote(packed.at[x], rc.at[x], c_send.at[0], c_recv.at[0], mate).wait_recv()
    rx[x] = packed[core * 4 + own] + rc[x]
    for o in FAR_4:
        source = lax.rem(x + NX - o, NX)
        remote(sum4.at[source], rx.at[source], x_send.at[o], x_recv.at[o], x_peers[o]).wait_recv()
    mine = (rx[0] + rx[1]) + (rx[2] + rx[3])

    for i in range(NZ):
        pz[i, 0:16, :] = mine[16 * i : 16 * i + 16]
        pz[i, 16:24, :] = mine[128:136]
    for o in FAR_8:
        zo = lax.rem(z + o, NZ)
        copy = remote(pz.at[zo], rz.at[z], z_send.at[o], z_recv.at[o], z_peers[o])
        copy.start()
        sends.append(copy)
    rz[z] = pz[z]
    for o in FAR_8:
        source = lax.rem(z + NZ - o, NZ)
        remote(pz.at[source], rz.at[source], z_send.at[o], z_recv.at[o], z_peers[o]).wait_recv()
    piece[...] = ((rz[0] + rz[1]) + (rz[2] + rz[3])) + ((rz[4] + rz[5]) + (rz[6] + rz[7]))

    for o in FAR_8:
        copy = remote(piece, ry.at[yy], y_send.at[o], y_recv.at[o], y_peers[o])
        copy.start()
        sends.append(copy)
    ry[yy] = piece[...]
    for o in FAR_8:
        source = lax.rem(yy + NY - o, NY)
        remote(piece, ry.at[source], y_send.at[o], y_recv.at[o], y_peers[o]).wait_recv()
    fin[...] = ((ry[0] + ry[1]) + (ry[2] + ry[3])) + ((ry[4] + ry[5]) + (ry[6] + ry[7]))

    for o in FAR_8:
        copy = remote(fin, gz.at[z], w_send.at[o], w_recv.at[o], z_peers[o])
        copy.start()
        sends.append(copy)
    gz[z] = fin[...]
    for o in FAR_8:
        source = lax.rem(z + NZ - o, NZ)
        remote(fin, gz.at[source], w_send.at[o], w_recv.at[o], z_peers[o]).wait_recv()
    slot = core * 4 + own
    factor(total_rows, gz, held, slot)

    half = (pl.ds(0, 64), pl.ds(64, 64))
    ways = (
        (0, pl.ds(0, 128), x_peers[2], 2),
        (1, half[0], line[2], 2),
        (1, half[1], line[6], 2),
        (0, pl.ds(0, 128), x_peers[1], 3),
        (0, pl.ds(0, 128), x_peers[3], 1),
        (1, pl.ds(0, 128), line[1], 3),
        (1, pl.ds(0, 128), line[7], 1),
    )
    for n, (k, rows, peer, _) in enumerate(ways):
        part = held.at[slot, k, rows]
        copy = remote(part, part, f_send.at[n], f_recv.at[n], peer)
        copy.start()
        sends.append(copy)
    copy = remote(held.at[slot], held.at[slot], m_send.at[7], m_recv.at[7], mate)
    copy.start()
    sends.append(copy)
    order = (3, 4, 5, 6, 0, 1, 2)
    for n in order:
        k, rows, peer, back = ways[n]
        part = held.at[core * 4 + lax.rem(own + back, NX), k, rows]
        remote(part, part, f_send.at[n], f_recv.at[n], peer).wait_recv()
        copy = remote(part, part, m_send.at[n], m_recv.at[n], mate)
        copy.start()
        sends.append(copy)
    theirs = held.at[(1 - core) * 4 + own]
    remote(theirs, theirs, m_send.at[7], m_recv.at[7], mate).wait_recv()
    for n in order:
        k, rows, peer, back = ways[n]
        part = held.at[(1 - core) * 4 + lax.rem(own + back, NX), k, rows]
        remote(part, part, m_send.at[n], m_recv.at[n], mate).wait_recv()
    out[...] = held[...]

    for copy in sends:
        copy.wait_send()
    save.wait()


def over_lanes(a, j):
    return jnp.broadcast_to(a[:, :, j : j + 1], a.shape)


def over_rows(a, i):
    return jnp.broadcast_to(a[:, i : i + 1, :], a.shape)


def factor(total_rows, g, held, slot):
    lanes, subs = iota((1, 8, 128), 2), iota((1, 8, 128), 1)
    row, col = iota((128, 128), 0), iota((128, 128), 1)
    square = jnp.concatenate([g[i, 0:16, :] for i in range(NZ)], axis=0) * (1.0 / total_rows)
    spare = g[0, 16:17, :] * (1.0 / total_rows)
    turned = square.T
    first = jnp.where(row == col, spare, jnp.where(row > col, square, turned))
    second = jnp.where(row > col, turned, square)
    m = [jnp.stack([first[8 * v : 8 * v + 8], second[8 * v : 8 * v + 8]]) for v in range(16)]
    for p in range(16):
        j0 = 8 * p
        top = m[p]
        here = (lanes >= j0) & (lanes < j0 + 8)
        columns = [over_lanes(top, j0 + k) for k in range(8)]
        a = [[over_rows(columns[k], i) for k in range(i + 1)] for i in range(8)]
        for k in range(8):
            r = lax.rsqrt(a[k][k])
            for q in range(k):
                a[k][q] = a[k][q] * r
            a[k][k] = r
            lower = {i: a[i][k] * r for i in range(k + 1, 8)}
            for i in range(k + 1, 8):
                for q in range(k):
                    a[i][q] = a[i][q] - lower[i] * a[k][q]
                a[i][k] = -(lower[i] * r)
                for q in range(k + 1, i + 1):
                    a[i][q] = a[i][q] - lower[i] * lower[q]

        def through(rows):
            done = []
            for i in range(8):
                total = a[i][0] * rows[0]
                for k in range(1, i + 1):
                    total = total + a[i][k] * rows[k]
                done.append(total)
            return done

        def joined(rows):
            whole = rows[7]
            for i in range(7):
                whole = jnp.where(subs == i, rows[i], whole)
            return whole

        base = jnp.where(here, jnp.where(lanes - j0 == subs, 1.0, 0.0), top)
        across = through([over_rows(base, k) for k in range(8)])
        corner = joined(through([over_rows(top, k) for k in range(8)]))
        m[p] = jnp.where(here & (lanes > j0 + subs), corner, joined(across))
        for v in range(p + 1, 16):
            left = through([over_lanes(m[v], j0 + k) for k in range(8)])
            rest = jnp.where(here, 0.0, m[v])
            for i in range(8):
                rest = rest - left[i] * across[i]
            m[v] = rest
    for v in range(16):
        held[slot, :, 8 * v : 8 * v + 8, :] = m[v]


def apply_kernel(pk, zz, upper, basis):
    row, col = iota((128, 128), 0), iota((128, 128), 1)
    for k in range(2):
        both = pk[0, k]
        upper[k] = jnp.where(col > row, both, jnp.where(col == row, 1.0 / both, 0.0))
        inverse = jnp.where(col <= row, both, 0.0)
        high = inverse.astype(BF16)
        low = (inverse - high.astype(F32)).astype(BF16)
        twice = jnp.concatenate([high, high], axis=1)
        found = dot(twice, zz[k]) + dot(low, zz[k, 0:128, :])
        for c in range(3):
            basis[k, c] = found[:, 128 * c : 128 * c + 128].astype(BF16)


def shards(strain, block_starts, bin_numbers):
    vmem = pl.BlockSpec(memory_space=pltpu.VMEM)
    smem = pl.BlockSpec(memory_space=pltpu.SMEM)
    hbm = pl.BlockSpec(memory_space=pl.ANY)
    dma = pltpu.SemaphoreType.DMA
    total_rows = 3.0 * 128 * lax.axis_size("space") * lax.axis_size("tm")
    zz, held = pl.pallas_call(
        functools.partial(first_kernel, total_rows),
        out_shape=(
            jax.ShapeDtypeStruct((16, 256, 384), BF16),
            jax.ShapeDtypeStruct((8, 2, 128, 128), F32),
        ),
        in_specs=[hbm, smem, smem],
        out_specs=(hbm, vmem),
        scratch_shapes=[
            pltpu.VMEM((NT, 3, 264, 128), BF16),
            pltpu.VMEM((8, 384, 128), BF16),
            pltpu.VMEM((256, 512), BF16),
            pltpu.VMEM((8, 256, 384), BF16),
            pltpu.VMEM((32, 64, 128), F32),
            pltpu.VMEM((16, 256, 384), BF16),
            pltpu.VMEM((16, 128, 128), F32),
            pltpu.VMEM((8, 136, 128), F32),
            pltpu.VMEM((4, 136, 128), F32),
            pltpu.VMEM((4, 136, 128), F32),
            pltpu.VMEM((4, 136, 128), F32),
            pltpu.VMEM((NZ, 24, 128), F32),
            pltpu.VMEM((NZ, 24, 128), F32),
            pltpu.VMEM((24, 128), F32),
            pltpu.VMEM((NY, 24, 128), F32),
            pltpu.VMEM((24, 128), F32),
            pltpu.VMEM((NZ, 24, 128), F32),
            pltpu.VMEM((8, 2, 128, 128), F32),
            dma((NT, 3)), dma((NT, 3)), dma,
            dma((4,)), dma((4,)), dma((4,)), dma((4,)),
            dma((8,)), dma((8,)), dma((8,)), dma((8,)), dma((8,)), dma((8,)),
            dma((7,)), dma((7,)), dma((8,)), dma((8,)), dma,
        ],
        compiler_params=pltpu.CompilerParams(
            collective_id=0, has_side_effects=True, vmem_limit_bytes=60 * 1024 * 1024
        ),
    )(strain, block_starts, bin_numbers)
    upper, basis = pl.pallas_call(
        apply_kernel,
        grid=(8,),
        out_shape=(
            jax.ShapeDtypeStruct((16, 128, 128), F32),
            jax.ShapeDtypeStruct((16, 3, 128, 128), BF16),
        ),
        in_specs=[
            pl.BlockSpec((1, 2, 128, 128), lambda i: (i, 0, 0, 0)),
            pl.BlockSpec((2, 256, 384), lambda i: (i, 0, 0)),
        ],
        out_specs=(
            pl.BlockSpec((2, 128, 128), lambda i: (i, 0, 0)),
            pl.BlockSpec((2, 3, 128, 128), lambda i: (i, 0, 0, 0)),
        ),
    )(held, zz)
    return upper, jnp.transpose(basis, (0, 2, 1, 3))


def solution(mesh):
    placed = (P(None, "tm", "space"), P(), P())
    return jax.shard_map(
        shards,
        mesh=mesh,
        in_specs=placed,
        out_specs=(P(), P(None, None, None, ("space", "tm"))),
        check_vma=False,
    )
```

```python
import functools
import math

import jax
import jax.numpy as jnp
from jax import lax
from jax.experimental import pallas as pl
from jax.experimental.pallas import tpu as pltpu
from jax.sharding import PartitionSpec as P

NFFT = 64
HOP = 32
MESH = pl.DeviceIdType.MESH
F32 = jnp.float32
BF16 = jnp.bfloat16

NX, NZ, NY, NT = 4, 8, 8, 8


def iota(shape, dim):
    return lax.broadcasted_iota(jnp.int32, shape, dim)


def dot(a, b):
    return jnp.dot(a, b, preferred_element_type=F32)


def dot_t(a, b):
    return lax.dot_general(a, b, (((1,), (1,)), ((), ())), preferred_element_type=F32)


def place():
    s, t = lax.axis_index("space"), lax.axis_index("tm")
    x = lax.rem(s, NX)
    z = lax.rem(lax.div(s, NX), NZ)
    ylo = lax.div(s, NX * NZ)
    core = lax.rem(t, 2)
    yhi = lax.div(t, 2)
    return s, t, x, z, ylo, core, yhi


def space_of(x, z, ylo):
    return (ylo * NZ + z) * NX + x


def remote(src, dst, send, recv, device):
    return pltpu.make_async_remote_copy(
        src_ref=src, dst_ref=dst, send_sem=send, recv_sem=recv,
        device_id=device, device_id_type=MESH,
    )


FAR_T = ((2, 0), (2, 1), (1, 0), (1, 1), (3, 0), (3, 1), (0, 1))
FAR_8 = (4, 3, 5, 2, 6, 1, 7)
FAR_4 = (2, 1, 3)


def build_windows(starts, bins, amat, mmat):
    step = iota((32, NFFT), 1)
    freq = lax.div(iota((32, NFFT), 0), 2)
    turns = jnp.zeros((32, NFFT), jnp.int32)
    for f in range(16):
        turns = jnp.where(freq == f, bins[f], turns)
    angle = (2.0 * math.pi) * lax.rem(turns * step, NFFT).astype(F32) / NFFT
    taper = (1.0 - jnp.cos((2.0 * math.pi) * step.astype(F32) / NFFT)) / math.sqrt(1.5 * NFFT)
    real = lax.rem(iota((32, NFFT), 0), 2) == 0
    window = (taper * jnp.where(real, jnp.cos(angle), -jnp.sin(angle))).astype(BF16)
    tile = (lax.rem(iota((NFFT, 512), 1), NFFT) == iota((NFFT, 512), 0)).astype(BF16)
    tiled = dot(window, tile).astype(BF16)
    spread = (lax.div(iota((256, 32), 0), 8) == iota((256, 32), 1)).astype(BF16)
    full = dot(spread, tiled)
    same = lax.rem(iota((256, 512), 0), 8) == lax.div(iota((256, 512), 1), NFFT)
    amat[...] = jnp.where(same, full, 0.0).astype(BF16)
    slot = iota((NFFT, 384), 1)
    when = jnp.where(slot < 264, slot, jnp.where(slot < 304, slot - 8, slot - 376))
    known = (slot < 264) | ((slot >= 272) & (slot < 304)) | ((slot >= 304) & (slot < 376))
    when = jnp.where(known, when, -100000) - iota((NFFT, 384), 0)
    for g in range(8):
        parts = []
        for b in range(8):
            begin = starts[8 * g + b] - 264 * g
            parts.append(jnp.where(when == begin, 1.0, 0.0).astype(BF16))
        pick = jnp.concatenate(parts, axis=0)
        mmat[g] = dot(amat[...], pick).astype(BF16)


def first_kernel(
    total_rows,     strain, starts, bins, zout, out,
    came, slab, amat, mmat, spec, zbuf, gram, packed, rc, sum4, rx, pz, rz, piece, ry, fin, gz, held,
    a_send, a_recv, own_sem, c_send, c_recv, x_send, x_recv, z_send, z_recv,
    y_send, y_recv, w_send, w_recv, f_send, f_recv, m_send, m_recv, out_sem, keep_sem,
):
    s, t, x, z, ylo, core, yhi = place()
    yy = yhi * 2 + ylo
    def tm_peer(dy, dc):
        return lax.rem(yhi + dy, 4) * 2 + lax.rem(core + dc, 2)

    tm_peers = [(s, tm_peer(*o)) for o in FAR_T]
    x_peers = {o: (space_of(lax.rem(x + o, NX), z, ylo), t) for o in FAR_4}
    z_peers = {o: (space_of(lax.rem(x + 8 - o, NX), lax.rem(z + o, NZ), ylo), t) for o in FAR_8}
    line = {o: (space_of(x, lax.rem(z + o, NZ), ylo), t) for o in (1, 2, 6, 7)}
    own = lax.rem(x + z, NX)

    def y_peer(o):
        other = lax.rem(yy + o, NY)
        return (space_of(x, z, lax.rem(other, 2)), lax.div(other, 2) * 2 + core)

    y_peers = {o: y_peer(o) for o in FAR_8}
    mate = (s, t + 1 - 2 * core)

    barrier = pltpu.get_barrier_semaphore()
    odd = {o: y_peers[o] for o in (1, 3, 5, 7)}
    greeted = tm_peers + list(x_peers.values()) + list(z_peers.values()) + list(odd.values()) + list(line.values())
    for peer in greeted:
        pl.semaphore_signal(barrier, inc=1, device_id=peer, device_id_type=MESH)
    pl.semaphore_wait(barrier, len(greeted))

    sends = []
    for c in range(3):
        for o in FAR_T:
            to = tm_peer(*o)
            n = o[0] * 2 + o[1]
            copy = remote(
                strain.at[c, :, pl.ds(pl.multiple_of(to * 128, 128), 128)],
                came.at[t, c], a_send.at[n, c], a_recv.at[n, c], (s, to),
            )
            copy.start()
            sends.append(copy)
    stay = pltpu.make_async_copy(
        strain.at[:, :, pl.ds(pl.multiple_of(t * 128, 128), 128)], came.at[t], own_sem
    )
    stay.start()

    build_windows(starts, bins, amat, mmat)
    slab[...] = jnp.zeros_like(slab)
    stay.wait()

    def square(c, f):
        rows = spec[pl.ds(2 * f, 2)].reshape(128, 128)
        high = rows.astype(BF16)
        low = (rows - high.astype(F32)).astype(BF16)
        both = jnp.concatenate([high, low], axis=0)
        zbuf[f, :, 128 * c : 128 * c + 128] = both
        quad = dot_t(both, both)
        return (quad[:128, :128] + quad[128:, 128:]) + (quad[:128, 128:] + quad[128:, :128])

    def product(c, f, carry):
        new = square(c, f)
        gram[f] = gram[f] + new if c else new
        return carry

    for c in range(3):
        for o in FAR_T:
            source = tm_peer(4 - o[0], o[1])
            n = o[0] * 2 + o[1]
            remote(
                came.at[source, c], came.at[source, c], a_send.at[n, c], a_recv.at[n, c], (s, source)
            ).wait_recv()
        for g in range(8):
            slab[g, 0:264, :] = came[g, c, :, :]
            if g < 7:
                slab[g, 272:304, :] = came[g + 1, c, 0:32, :]
            if g > 0:
                slab[g, 304:376, :] = came[g - 1, c, 192:264, :]
        for g in range(8):
            found = dot(mmat[g], slab[g])
            spec[:, 8 * g : 8 * g + 8, :] = found.reshape(32, 8, 128)

        if c < 2:
            lax.fori_loop(0, 16, functools.partial(product, c), 0)

    row, col = iota((128, 128), 0), iota((128, 128), 1)

    def finish(q):
        first = gram[2 * q] + square(2, 2 * q)
        second = gram[2 * q + 1] + square(2, 2 * q + 1)
        packed[q, 0:128, :] = jnp.where(row > col, first, second)
        diag = jnp.sum(jnp.where(row == col, first, 0.0), axis=0, keepdims=True)
        packed[q, 128:136, :] = jnp.broadcast_to(diag, (8, 128))

    there = {o: lax.rem(x + o, NX) for o in FAR_4 + (0,)}
    theirs = {o: (1 - core) * 4 + lax.rem(there[o] + z, NX) for o in there}
    ours = {o: core * 4 + lax.rem(there[o] + z, NX) for o in there}
    for o in there:
        finish(theirs[o])
    for o in there:
        copy = remote(packed.at[theirs[o]], rc.at[there[o]], c_send.at[o], c_recv.at[o], mate)
        copy.start()
        sends.append(copy)
    for o in there:
        finish(ours[o])
    for o in there:
        xo, pair = there[o], ours[o]
        remote(packed.at[pair], rc.at[xo], c_send.at[o], c_recv.at[o], mate).wait_recv()
        if o:
            sum4[xo] = packed[pair] + rc[xo]
            copy = remote(sum4.at[xo], rx.at[x], x_send.at[o], x_recv.at[o], x_peers[o])
            copy.start()
            sends.append(copy)
        else:
            rx[x] = packed[pair] + rc[x]
    save = pltpu.make_async_copy(zbuf, zout, out_sem)
    save.start()
    for o in FAR_4:
        source = lax.rem(x + NX - o, NX)
        remote(sum4.at[source], rx.at[source], x_send.at[o], x_recv.at[o], x_peers[o]).wait_recv()
    mine = (rx[0] + rx[1]) + (rx[2] + rx[3])

    for i in range(NZ):
        pz[i, 0:16, :] = mine[16 * i : 16 * i + 16]
        pz[i, 16:24, :] = mine[128:136]
    for o in FAR_8:
        zo = lax.rem(z + o, NZ)
        copy = remote(pz.at[zo], rz.at[z], z_send.at[o], z_recv.at[o], z_peers[o])
        copy.start()
        sends.append(copy)
    rz[z] = pz[z]
    for o in FAR_8:
        source = lax.rem(z + NZ - o, NZ)
        remote(pz.at[source], rz.at[source], z_send.at[o], z_recv.at[o], z_peers[o]).wait_recv()
    piece[...] = ((rz[0] + rz[1]) + (rz[2] + rz[3])) + ((rz[4] + rz[5]) + (rz[6] + rz[7]))

    for o in FAR_8:
        copy = remote(piece, ry.at[yy], y_send.at[o], y_recv.at[o], y_peers[o])
        copy.start()
        sends.append(copy)
    ry[yy] = piece[...]
    for o in FAR_8:
        source = lax.rem(yy + NY - o, NY)
        remote(piece, ry.at[source], y_send.at[o], y_recv.at[o], y_peers[o]).wait_recv()
    fin[...] = ((ry[0] + ry[1]) + (ry[2] + ry[3])) + ((ry[4] + ry[5]) + (ry[6] + ry[7]))

    for o in FAR_8:
        copy = remote(fin, gz.at[z], w_send.at[o], w_recv.at[o], z_peers[o])
        copy.start()
        sends.append(copy)
    gz[z] = fin[...]
    for o in FAR_8:
        source = lax.rem(z + NZ - o, NZ)
        remote(fin, gz.at[source], w_send.at[o], w_recv.at[o], z_peers[o]).wait_recv()
    slot = core * 4 + own
    ways = []
    for band, (start, size) in enumerate(((0, 64), (64, 32), (96, 32))):
        rows = pl.ds(start, size)
        if band == 0:
            ways.append((band, 1, pl.ds(0, 32), line[2], 2))
            ways.append((band, 1, pl.ds(32, 32), line[6], 2))
        else:
            ways.append((band, 1, rows, line[2 if band == 1 else 6], 2))
        ways.append((band, 0, rows, x_peers[2], 2))
        ways.append((band, 0, rows, x_peers[1], 3))
        ways.append((band, 0, rows, x_peers[3], 1))
        ways.append((band, 1, rows, line[1], 3))
        ways.append((band, 1, rows, line[7], 1))
    bands = (pl.ds(0, 64), pl.ds(64, 32), pl.ds(96, 32))

    def final(band):
        for n, (which, k, rows, peer, _) in enumerate(ways):
            if which == band:
                part = held.at[slot, k, rows]
                copy = remote(part, part, f_send.at[n], f_recv.at[n], peer)
                copy.start()
                sends.append(copy)
        part = held.at[slot, :, bands[band]]
        copy = remote(part, part, m_send.at[20 + band], m_recv.at[20 + band], mate)
        copy.start()
        sends.append(copy)

    factor(total_rows, gz, held, slot, final)

    order = [n for band in range(3) for d in (3, 1, 2) for n, w in enumerate(ways) if w[0] == band and w[4] == d]
    for n in order:
        _, k, rows, peer, back = ways[n]
        part = held.at[core * 4 + lax.rem(own + back, NX), k, rows]
        remote(part, part, f_send.at[n], f_recv.at[n], peer).wait_recv()
        copy = remote(part, part, m_send.at[n], m_recv.at[n], mate)
        copy.start()
        sends.append(copy)
    keep = [
        pltpu.make_async_copy(held.at[pl.ds(q * 4, 4)], out.at[pl.ds(q * 4, 4)], keep_sem.at[n])
        for n, q in enumerate((core, 1 - core))
    ]
    keep[0].start()
    for band in range(3):
        part = held.at[(1 - core) * 4 + own, :, bands[band]]
        remote(part, part, m_send.at[20 + band], m_recv.at[20 + band], mate).wait_recv()
    for n in order:
        _, k, rows, peer, back = ways[n]
        part = held.at[(1 - core) * 4 + lax.rem(own + back, NX), k, rows]
        remote(part, part, m_send.at[n], m_recv.at[n], mate).wait_recv()
    keep[1].start()

    for copy in sends:
        copy.wait_send()
    save.wait()
    for copy in keep:
        copy.wait()


def over_lanes(a, j):
    return jnp.broadcast_to(a[:, :, j : j + 1], a.shape)


def over_rows(a, i):
    return jnp.broadcast_to(a[:, i : i + 1, :], a.shape)


def factor(total_rows, g, held, slot, final):
    lanes, subs = iota((1, 8, 128), 2), iota((1, 8, 128), 1)
    row, col = iota((128, 128), 0), iota((128, 128), 1)
    square = jnp.concatenate([g[i, 0:16, :] for i in range(NZ)], axis=0) * (1.0 / total_rows)
    spare = g[0, 16:17, :] * (1.0 / total_rows)
    turned = square.T
    first = jnp.where(row == col, spare, jnp.where(row > col, square, turned))
    second = jnp.where(row > col, turned, square)
    m = [jnp.stack([first[8 * v : 8 * v + 8], second[8 * v : 8 * v + 8]]) for v in range(16)]
    for p in range(16):
        j0 = 8 * p
        top = m[p]
        here = (lanes >= j0) & (lanes < j0 + 8)
        columns = [over_lanes(top, j0 + k) for k in range(8)]
        a = [[over_rows(columns[k], i) for k in range(i + 1)] for i in range(8)]
        for k in range(8):
            r = lax.rsqrt(a[k][k])
            for q in range(k):
                a[k][q] = a[k][q] * r
            a[k][k] = r
            lower = {i: a[i][k] * r for i in range(k + 1, 8)}
            for i in range(k + 1, 8):
                for q in range(k):
                    a[i][q] = a[i][q] - lower[i] * a[k][q]
                a[i][k] = -(lower[i] * r)
                for q in range(k + 1, i + 1):
                    a[i][q] = a[i][q] - lower[i] * lower[q]

        def through(rows):
            done = []
            for i in range(8):
                total = a[i][0] * rows[0]
                for k in range(1, i + 1):
                    total = total + a[i][k] * rows[k]
                done.append(total)
            return done

        def joined(rows):
            whole = rows[7]
            for i in range(7):
                whole = jnp.where(subs == i, rows[i], whole)
            return whole

        base = jnp.where(here, jnp.where(lanes - j0 == subs, 1.0, 0.0), top)
        across = through([over_rows(base, k) for k in range(8)])
        corner = joined(through([over_rows(top, k) for k in range(8)]))
        held[slot, :, j0 : j0 + 8, :] = jnp.where(here & (lanes > j0 + subs), corner, joined(across))
        if p in (7, 11, 15):
            final((7, 11, 15).index(p))
        for v in range(p + 1, 16):
            left = through([over_lanes(m[v], j0 + k) for k in range(8)])
            rest = jnp.where(here, 0.0, m[v])
            for i in range(8):
                rest = rest - left[i] * across[i]
            m[v] = rest

def apply_kernel(pk, zz, upper, basis):
    row, col = iota((128, 128), 0), iota((128, 128), 1)
    for k in range(8):
        both = pk[k // 2, k % 2]
        upper[k] = jnp.where(col > row, both, jnp.where(col == row, 1.0 / both, 0.0))
        inverse = jnp.where(col <= row, both, 0.0)
        high = inverse.astype(BF16)
        low = (inverse - high.astype(F32)).astype(BF16)
        twice = jnp.concatenate([high, high], axis=1)
        found = dot(twice, zz[k]) + dot(low, zz[k, 0:128, :])
        for c in range(3):
            basis[k, c] = found[:, 128 * c : 128 * c + 128].astype(BF16)


def shards(strain, block_starts, bin_numbers):
    smem = pl.BlockSpec(memory_space=pltpu.SMEM)
    hbm = pl.BlockSpec(memory_space=pl.ANY)
    dma = pltpu.SemaphoreType.DMA
    total_rows = 3.0 * 128 * lax.axis_size("space") * lax.axis_size("tm")
    zz, held = pl.pallas_call(
        functools.partial(first_kernel, total_rows),
        out_shape=(
            jax.ShapeDtypeStruct((16, 256, 384), BF16),
            jax.ShapeDtypeStruct((8, 2, 128, 128), F32),
        ),
        in_specs=[hbm, smem, smem],
        out_specs=(hbm, hbm),
        scratch_shapes=[
            pltpu.VMEM((NT, 3, 264, 128), BF16),
            pltpu.VMEM((8, 384, 128), BF16),
            pltpu.VMEM((256, 512), BF16),
            pltpu.VMEM((8, 256, 384), BF16),
            pltpu.VMEM((32, 64, 128), F32),
            pltpu.VMEM((16, 256, 384), BF16),
            pltpu.VMEM((16, 128, 128), F32),
            pltpu.VMEM((8, 136, 128), F32),
            pltpu.VMEM((4, 136, 128), F32),
            pltpu.VMEM((4, 136, 128), F32),
            pltpu.VMEM((4, 136, 128), F32),
            pltpu.VMEM((NZ, 24, 128), F32),
            pltpu.VMEM((NZ, 24, 128), F32),
            pltpu.VMEM((24, 128), F32),
            pltpu.VMEM((NY, 24, 128), F32),
            pltpu.VMEM((24, 128), F32),
            pltpu.VMEM((NZ, 24, 128), F32),
            pltpu.VMEM((8, 2, 128, 128), F32),
            dma((NT, 3)), dma((NT, 3)), dma,
            dma((4,)), dma((4,)), dma((4,)), dma((4,)),
            dma((8,)), dma((8,)), dma((8,)), dma((8,)), dma((8,)), dma((8,)),
            dma((20,)), dma((20,)), dma((23,)), dma((23,)), dma, dma((2,)),
        ],
        compiler_params=pltpu.CompilerParams(
            collective_id=0, has_side_effects=True, vmem_limit_bytes=60 * 1024 * 1024
        ),
    )(strain, block_starts, bin_numbers)
    upper, basis = pl.pallas_call(
        apply_kernel,
        grid=(2,),
        out_shape=(
            jax.ShapeDtypeStruct((16, 128, 128), F32),
            jax.ShapeDtypeStruct((16, 3, 128, 128), BF16),
        ),
        in_specs=[
            pl.BlockSpec((4, 2, 128, 128), lambda i: (i, 0, 0, 0)),
            pl.BlockSpec((8, 256, 384), lambda i: (i, 0, 0)),
        ],
        out_specs=(
            pl.BlockSpec((8, 128, 128), lambda i: (i, 0, 0)),
            pl.BlockSpec((8, 3, 128, 128), lambda i: (i, 0, 0, 0)),
        ),
        compiler_params=pltpu.CompilerParams(vmem_limit_bytes=32 * 1024 * 1024),
    )(held, zz)
    return upper, jnp.transpose(basis, (0, 2, 1, 3))


def solution(mesh):
    placed = (P(None, "tm", "space"), P(), P())
    return jax.shard_map(
        shards,
        mesh=mesh,
        in_specs=placed,
        out_specs=(P(), P(None, None, None, ("space", "tm"))),
        check_vma=False,
    )
```

```python
import functools
import math

import jax
import jax.numpy as jnp
from jax import lax
from jax.experimental import pallas as pl
from jax.experimental.pallas import tpu as pltpu
from jax.sharding import PartitionSpec as P

NFFT = 64
HOP = 32
MESH = pl.DeviceIdType.MESH
F32 = jnp.float32
BF16 = jnp.bfloat16

NX, NZ, NY, NT = 4, 8, 8, 8


def iota(shape, dim):
    return lax.broadcasted_iota(jnp.int32, shape, dim)


def dot(a, b):
    return jnp.dot(a, b, preferred_element_type=F32)


def dot_t(a, b):
    return lax.dot_general(a, b, (((1,), (1,)), ((), ())), preferred_element_type=F32)


def place():
    s, t = lax.axis_index("space"), lax.axis_index("tm")
    x = lax.rem(s, NX)
    z = lax.rem(lax.div(s, NX), NZ)
    ylo = lax.div(s, NX * NZ)
    core = lax.rem(t, 2)
    yhi = lax.div(t, 2)
    return s, t, x, z, ylo, core, yhi


def space_of(x, z, ylo):
    return (ylo * NZ + z) * NX + x


def remote(src, dst, send, recv, device):
    return pltpu.make_async_remote_copy(
        src_ref=src, dst_ref=dst, send_sem=send, recv_sem=recv,
        device_id=device, device_id_type=MESH,
    )


FAR_T = ((2, 0), (2, 1), (1, 0), (1, 1), (3, 0), (3, 1), (0, 1))
FAR_8 = (4, 3, 5, 2, 6, 1, 7)
FAR_4 = (2, 1, 3)


def build_windows(starts, bins, amat, mmat):
    step = iota((32, NFFT), 1)
    freq = lax.div(iota((32, NFFT), 0), 2)
    turns = jnp.zeros((32, NFFT), jnp.int32)
    for f in range(16):
        turns = jnp.where(freq == f, bins[f], turns)
    angle = (2.0 * math.pi) * lax.rem(turns * step, NFFT).astype(F32) / NFFT
    taper = (1.0 - jnp.cos((2.0 * math.pi) * step.astype(F32) / NFFT)) / math.sqrt(1.5 * NFFT)
    real = lax.rem(iota((32, NFFT), 0), 2) == 0
    window = (taper * jnp.where(real, jnp.cos(angle), -jnp.sin(angle))).astype(BF16)
    tile = (lax.rem(iota((NFFT, 512), 1), NFFT) == iota((NFFT, 512), 0)).astype(BF16)
    tiled = dot(window, tile).astype(BF16)
    spread = (lax.div(iota((256, 32), 0), 8) == iota((256, 32), 1)).astype(BF16)
    full = dot(spread, tiled)
    same = lax.rem(iota((256, 512), 0), 8) == lax.div(iota((256, 512), 1), NFFT)
    amat[...] = jnp.where(same, full, 0.0).astype(BF16)
    slot = iota((NFFT, 384), 1)
    when = jnp.where(slot < 264, slot, jnp.where(slot < 304, slot - 8, slot - 376))
    known = (slot < 264) | ((slot >= 272) & (slot < 304)) | ((slot >= 304) & (slot < 376))
    when = jnp.where(known, when, -100000) - iota((NFFT, 384), 0)
    for g in range(8):
        parts = []
        for b in range(8):
            begin = starts[8 * g + b] - 264 * g
            parts.append(jnp.where(when == begin, 1.0, 0.0).astype(BF16))
        pick = jnp.concatenate(parts, axis=0)
        mmat[g] = dot(amat[...], pick).astype(BF16)


def first_kernel(
    total_rows,     strain, starts, bins, zout, out,
    came, slab, amat, mmat, spec, zbuf, gram, packed, rc, sum4, rx, pz, rz, piece, ry, fin, gz, held,
    a_send, a_recv, own_sem, c_send, c_recv, x_send, x_recv, z_send, z_recv,
    y_send, y_recv, w_send, w_recv, f_send, f_recv, m_send, m_recv, out_sem, keep_sem,
):
    s, t, x, z, ylo, core, yhi = place()
    yy = yhi * 2 + ylo
    def tm_peer(dy, dc):
        return lax.rem(yhi + dy, 4) * 2 + lax.rem(core + dc, 2)

    tm_peers = [(s, tm_peer(*o)) for o in FAR_T]
    x_peers = {o: (space_of(lax.rem(x + o, NX), z, ylo), t) for o in FAR_4}
    z_peers = {o: (space_of(lax.rem(x + 8 - o, NX), lax.rem(z + o, NZ), ylo), t) for o in FAR_8}
    line = {o: (space_of(x, lax.rem(z + o, NZ), ylo), t) for o in (1, 2, 6, 7)}
    own = lax.rem(x + z, NX)

    def y_peer(o):
        other = lax.rem(yy + o, NY)
        return (space_of(x, z, lax.rem(other, 2)), lax.div(other, 2) * 2 + core)

    y_peers = {o: y_peer(o) for o in FAR_8}
    mate = (s, t + 1 - 2 * core)

    barrier = pltpu.get_barrier_semaphore()
    odd = {o: y_peers[o] for o in (1, 3, 5, 7)}
    greeted = tm_peers + list(x_peers.values()) + list(z_peers.values()) + list(odd.values()) + list(line.values())
    for peer in greeted:
        pl.semaphore_signal(barrier, inc=1, device_id=peer, device_id_type=MESH)
    pl.semaphore_wait(barrier, len(greeted))

    sends = []
    for c in range(3):
        for o in FAR_T:
            to = tm_peer(*o)
            n = o[0] * 2 + o[1]
            copy = remote(
                strain.at[c, :, pl.ds(pl.multiple_of(to * 128, 128), 128)],
                came.at[t, c], a_send.at[n, c], a_recv.at[n, c], (s, to),
            )
            copy.start()
            sends.append(copy)
    stay = pltpu.make_async_copy(
        strain.at[:, :, pl.ds(pl.multiple_of(t * 128, 128), 128)], came.at[t], own_sem
    )
    stay.start()

    build_windows(starts, bins, amat, mmat)
    slab[...] = jnp.zeros_like(slab)
    stay.wait()

    def square(c, f):
        rows = spec[pl.ds(2 * f, 2)].reshape(128, 128)
        high = rows.astype(BF16)
        low = (rows - high.astype(F32)).astype(BF16)
        both = jnp.concatenate([high, low], axis=0)
        zbuf[f, :, 128 * c : 128 * c + 128] = both
        quad = dot_t(both, both)
        return (quad[:128, :128] + quad[128:, 128:]) + (quad[:128, 128:] + quad[128:, :128])

    def product(c, f, carry):
        new = square(c, f)
        gram[f] = gram[f] + new if c else new
        return carry

    for c in range(3):
        for o in FAR_T:
            source = tm_peer(4 - o[0], o[1])
            n = o[0] * 2 + o[1]
            remote(
                came.at[source, c], came.at[source, c], a_send.at[n, c], a_recv.at[n, c], (s, source)
            ).wait_recv()
        for g in range(8):
            slab[g, 0:264, :] = came[g, c, :, :]
            if g < 7:
                slab[g, 272:304, :] = came[g + 1, c, 0:32, :]
            if g > 0:
                slab[g, 304:376, :] = came[g - 1, c, 192:264, :]
        for g in range(8):
            found = dot(mmat[g], slab[g])
            spec[:, 8 * g : 8 * g + 8, :] = found.reshape(32, 8, 128)

        if c < 2:
            lax.fori_loop(0, 16, functools.partial(product, c), 0)

    row, col = iota((128, 128), 0), iota((128, 128), 1)

    def finish(q):
        first = gram[2 * q] + square(2, 2 * q)
        second = gram[2 * q + 1] + square(2, 2 * q + 1)
        packed[q, 0:128, :] = jnp.where(row > col, first, second)
        diag = jnp.sum(jnp.where(row == col, first, 0.0), axis=0, keepdims=True)
        packed[q, 128:136, :] = jnp.broadcast_to(diag, (8, 128))

    there = {o: lax.rem(x + o, NX) for o in FAR_4 + (0,)}
    theirs = {o: (1 - core) * 4 + lax.rem(there[o] + z, NX) for o in there}
    ours = {o: core * 4 + lax.rem(there[o] + z, NX) for o in there}
    for o in there:
        finish(theirs[o])
    for o in there:
        copy = remote(packed.at[theirs[o]], rc.at[there[o]], c_send.at[o], c_recv.at[o], mate)
        copy.start()
        sends.append(copy)
    for o in there:
        finish(ours[o])
    for o in there:
        xo, pair = there[o], ours[o]
        remote(packed.at[pair], rc.at[xo], c_send.at[o], c_recv.at[o], mate).wait_recv()
        if o:
            sum4[xo] = packed[pair] + rc[xo]
            copy = remote(sum4.at[xo], rx.at[x], x_send.at[o], x_recv.at[o], x_peers[o])
            copy.start()
            sends.append(copy)
        else:
            rx[x] = packed[pair] + rc[x]
    save = pltpu.make_async_copy(zbuf, zout, out_sem)
    save.start()
    for o in FAR_4:
        source = lax.rem(x + NX - o, NX)
        remote(sum4.at[source], rx.at[source], x_send.at[o], x_recv.at[o], x_peers[o]).wait_recv()
    mine = (rx[0] + rx[1]) + (rx[2] + rx[3])

    for i in range(NZ):
        pz[i, 0:16, :] = mine[16 * i : 16 * i + 16]
        pz[i, 16:24, :] = mine[128:136]
    for o in FAR_8:
        zo = lax.rem(z + o, NZ)
        copy = remote(pz.at[zo], rz.at[z], z_send.at[o], z_recv.at[o], z_peers[o])
        copy.start()
        sends.append(copy)
    rz[z] = pz[z]
    for o in FAR_8:
        source = lax.rem(z + NZ - o, NZ)
        remote(pz.at[source], rz.at[source], z_send.at[o], z_recv.at[o], z_peers[o]).wait_recv()
    piece[...] = ((rz[0] + rz[1]) + (rz[2] + rz[3])) + ((rz[4] + rz[5]) + (rz[6] + rz[7]))

    for o in FAR_8:
        copy = remote(piece, ry.at[yy], y_send.at[o], y_recv.at[o], y_peers[o])
        copy.start()
        sends.append(copy)
    ry[yy] = piece[...]
    for o in FAR_8:
        source = lax.rem(yy + NY - o, NY)
        remote(piece, ry.at[source], y_send.at[o], y_recv.at[o], y_peers[o]).wait_recv()
    fin[...] = ((ry[0] + ry[1]) + (ry[2] + ry[3])) + ((ry[4] + ry[5]) + (ry[6] + ry[7]))

    for o in FAR_8:
        copy = remote(fin.at[pl.ds(0, 16)], gz.at[z], w_send.at[o], w_recv.at[o], z_peers[o])
        copy.start()
        sends.append(copy)
    gz[z] = fin[0:16, :]
    for o in FAR_8:
        source = lax.rem(z + NZ - o, NZ)
        remote(fin.at[pl.ds(0, 16)], gz.at[source], w_send.at[o], w_recv.at[o], z_peers[o]).wait_recv()
    slot = core * 4 + own
    ways = []
    for band, (start, size) in enumerate(((0, 64), (64, 32), (96, 32))):
        rows = pl.ds(start, size)
        if band == 0:
            ways.append((band, 1, pl.ds(0, 32), line[2], 2))
            ways.append((band, 1, pl.ds(32, 32), line[6], 2))
        else:
            ways.append((band, 1, rows, line[2 if band == 1 else 6], 2))
        ways.append((band, 0, rows, x_peers[2], 2))
        ways.append((band, 0, rows, x_peers[1], 3))
        ways.append((band, 0, rows, x_peers[3], 1))
        ways.append((band, 1, rows, line[1], 3))
        ways.append((band, 1, rows, line[7], 1))
    bands = (pl.ds(0, 64), pl.ds(64, 32), pl.ds(96, 32))

    def final(band):
        for n, (which, k, rows, peer, _) in enumerate(ways):
            if which == band:
                part = held.at[slot, k, rows]
                copy = remote(part, part, f_send.at[n], f_recv.at[n], peer)
                copy.start()
                sends.append(copy)
        part = held.at[slot, :, bands[band]]
        copy = remote(part, part, m_send.at[20 + band], m_recv.at[20 + band], mate)
        copy.start()
        sends.append(copy)

    factor(total_rows, gz, fin, held, slot, final)

    order = [n for band in range(3) for d in (3, 1, 2) for n, w in enumerate(ways) if w[0] == band and w[4] == d]
    for n in order:
        _, k, rows, peer, back = ways[n]
        part = held.at[core * 4 + lax.rem(own + back, NX), k, rows]
        remote(part, part, f_send.at[n], f_recv.at[n], peer).wait_recv()
        copy = remote(part, part, m_send.at[n], m_recv.at[n], mate)
        copy.start()
        sends.append(copy)
    keep = [
        pltpu.make_async_copy(held.at[pl.ds(q * 4, 4)], out.at[pl.ds(q * 4, 4)], keep_sem.at[n])
        for n, q in enumerate((core, 1 - core))
    ]
    keep[0].start()
    for band in range(3):
        part = held.at[(1 - core) * 4 + own, :, bands[band]]
        remote(part, part, m_send.at[20 + band], m_recv.at[20 + band], mate).wait_recv()
    for n in order:
        _, k, rows, peer, back = ways[n]
        part = held.at[(1 - core) * 4 + lax.rem(own + back, NX), k, rows]
        remote(part, part, m_send.at[n], m_recv.at[n], mate).wait_recv()
    keep[1].start()

    for copy in sends:
        copy.wait_send()
    save.wait()
    for copy in keep:
        copy.wait()


def over_lanes(a, j):
    return jnp.broadcast_to(a[:, :, j : j + 1], a.shape)


def over_rows(a, i):
    return jnp.broadcast_to(a[:, i : i + 1, :], a.shape)


def factor(total_rows, g, fin, held, slot, final):
    lanes, subs = iota((1, 8, 128), 2), iota((1, 8, 128), 1)
    row, col = iota((128, 128), 0), iota((128, 128), 1)
    square = jnp.concatenate([g[i] for i in range(NZ)], axis=0) * (1.0 / total_rows)
    spare = fin[16:17, :] * (1.0 / total_rows)
    turned = square.T
    first = jnp.where(row == col, spare, jnp.where(row > col, square, turned))
    second = jnp.where(row > col, turned, square)
    m = [jnp.stack([first[8 * v : 8 * v + 8], second[8 * v : 8 * v + 8]]) for v in range(16)]
    for p in range(16):
        j0 = 8 * p
        top = m[p]
        here = (lanes >= j0) & (lanes < j0 + 8)
        columns = [over_lanes(top, j0 + k) for k in range(8)]
        a = [[over_rows(columns[k], i) for k in range(i + 1)] for i in range(8)]
        for k in range(8):
            r = lax.rsqrt(a[k][k])
            for q in range(k):
                a[k][q] = a[k][q] * r
            a[k][k] = r
            lower = {i: a[i][k] * r for i in range(k + 1, 8)}
            for i in range(k + 1, 8):
                for q in range(k):
                    a[i][q] = a[i][q] - lower[i] * a[k][q]
                a[i][k] = -(lower[i] * r)
                for q in range(k + 1, i + 1):
                    a[i][q] = a[i][q] - lower[i] * lower[q]

        def through(rows):
            done = []
            for i in range(8):
                total = a[i][0] * rows[0]
                for k in range(1, i + 1):
                    total = total + a[i][k] * rows[k]
                done.append(total)
            return done

        def joined(rows):
            whole = rows[7]
            for i in range(7):
                whole = jnp.where(subs == i, rows[i], whole)
            return whole

        base = jnp.where(here, jnp.where(lanes - j0 == subs, 1.0, 0.0), top)
        across = through([over_rows(base, k) for k in range(8)])
        corner = joined(through([over_rows(top, k) for k in range(8)]))
        held[slot, :, j0 : j0 + 8, :] = jnp.where(here & (lanes > j0 + subs), corner, joined(across))
        if p in (7, 11, 15):
            final((7, 11, 15).index(p))
        for v in range(p + 1, 16):
            left = through([over_lanes(m[v], j0 + k) for k in range(8)])
            rest = jnp.where(here, 0.0, m[v])
            for i in range(8):
                rest = rest - left[i] * across[i]
            m[v] = rest

def apply_kernel(pk, zz, upper, basis):
    row, col = iota((128, 128), 0), iota((128, 128), 1)
    step = pl.program_id(0)
    for k in range(8):
        both = pk[4 * step + k // 2, k % 2]
        upper[k] = jnp.where(col > row, both, jnp.where(col == row, 1.0 / both, 0.0))
        inverse = jnp.where(col <= row, both, 0.0)
        high = inverse.astype(BF16)
        low = (inverse - high.astype(F32)).astype(BF16)
        twice = jnp.concatenate([high, high], axis=1)
        found = dot(twice, zz[8 * step + k]) + dot(low, zz[8 * step + k, 0:128, :])
        for c in range(3):
            basis[k, c] = found[:, 128 * c : 128 * c + 128].astype(BF16)


def shards(strain, block_starts, bin_numbers):
    vmem = pl.BlockSpec(memory_space=pltpu.VMEM)
    smem = pl.BlockSpec(memory_space=pltpu.SMEM)
    hbm = pl.BlockSpec(memory_space=pl.ANY)
    dma = pltpu.SemaphoreType.DMA
    total_rows = 3.0 * 128 * lax.axis_size("space") * lax.axis_size("tm")
    zz, held = pl.pallas_call(
        functools.partial(first_kernel, total_rows),
        out_shape=(
            pltpu.VMEM((16, 256, 384), BF16),
            pltpu.VMEM((8, 2, 128, 128), F32),
        ),
        in_specs=[hbm, smem, smem],
        out_specs=(hbm, hbm),
        scratch_shapes=[
            pltpu.VMEM((NT, 3, 264, 128), BF16),
            pltpu.VMEM((8, 384, 128), BF16),
            pltpu.VMEM((256, 512), BF16),
            pltpu.VMEM((8, 256, 384), BF16),
            pltpu.VMEM((32, 64, 128), F32),
            pltpu.VMEM((16, 256, 384), BF16),
            pltpu.VMEM((16, 128, 128), F32),
            pltpu.VMEM((8, 136, 128), F32),
            pltpu.VMEM((4, 136, 128), F32),
            pltpu.VMEM((4, 136, 128), F32),
            pltpu.VMEM((4, 136, 128), F32),
            pltpu.VMEM((NZ, 24, 128), F32),
            pltpu.VMEM((NZ, 24, 128), F32),
            pltpu.VMEM((24, 128), F32),
            pltpu.VMEM((NY, 24, 128), F32),
            pltpu.VMEM((24, 128), F32),
            pltpu.VMEM((NZ, 16, 128), F32),
            pltpu.VMEM((8, 2, 128, 128), F32),
            dma((NT, 3)), dma((NT, 3)), dma,
            dma((4,)), dma((4,)), dma((4,)), dma((4,)),
            dma((8,)), dma((8,)), dma((8,)), dma((8,)), dma((8,)), dma((8,)),
            dma((20,)), dma((20,)), dma((23,)), dma((23,)), dma, dma((2,)),
        ],
        compiler_params=pltpu.CompilerParams(
            collective_id=0, has_side_effects=True, vmem_limit_bytes=58 * 1024 * 1024
        ),
    )(strain, block_starts, bin_numbers)
    upper, basis = pl.pallas_call(
        apply_kernel,
        grid=(2,),
        out_shape=(
            jax.ShapeDtypeStruct((16, 128, 128), F32),
            jax.ShapeDtypeStruct((16, 3, 128, 128), BF16),
        ),
        in_specs=[vmem, vmem],
        out_specs=(
            pl.BlockSpec((8, 128, 128), lambda i: (i, 0, 0)),
            pl.BlockSpec((8, 3, 128, 128), lambda i: (i, 0, 0, 0)),
        ),
        compiler_params=pltpu.CompilerParams(vmem_limit_bytes=24 * 1024 * 1024),
    )(held, zz)
    return upper, jnp.transpose(basis, (0, 2, 1, 3))


def solution(mesh):
    placed = (P(None, "tm", "space"), P(), P())
    return jax.shard_map(
        shards,
        mesh=mesh,
        in_specs=placed,
        out_specs=(P(), P(None, None, None, ("space", "tm"))),
        check_vma=False,
    )
```

```python
import functools
import math

import jax
import jax.numpy as jnp
from jax import lax
from jax.experimental import pallas as pl
from jax.experimental.pallas import tpu as pltpu
from jax.sharding import PartitionSpec as P

NFFT = 64
HOP = 32
MESH = pl.DeviceIdType.MESH
F32 = jnp.float32
BF16 = jnp.bfloat16

NX, NZ, NY, NT = 4, 8, 8, 8


def iota(shape, dim):
    return lax.broadcasted_iota(jnp.int32, shape, dim)


def dot(a, b):
    return jnp.dot(a, b, preferred_element_type=F32)


def dot_t(a, b):
    return lax.dot_general(a, b, (((1,), (1,)), ((), ())), preferred_element_type=F32)


def place():
    s, t = lax.axis_index("space"), lax.axis_index("tm")
    x = lax.rem(s, NX)
    z = lax.rem(lax.div(s, NX), NZ)
    ylo = lax.div(s, NX * NZ)
    core = lax.rem(t, 2)
    yhi = lax.div(t, 2)
    return s, t, x, z, ylo, core, yhi


def space_of(x, z, ylo):
    return (ylo * NZ + z) * NX + x


def remote(src, dst, send, recv, device):
    return pltpu.make_async_remote_copy(
        src_ref=src, dst_ref=dst, send_sem=send, recv_sem=recv,
        device_id=device, device_id_type=MESH,
    )


FAR_T = ((2, 0), (2, 1), (1, 0), (1, 1), (3, 0), (3, 1), (0, 1))
FAR_8 = (4, 3, 5, 2, 6, 1, 7)
FAR_4 = (2, 1, 3)


def build_windows(starts, bins, amat, mmat):
    step = iota((32, NFFT), 1)
    freq = lax.div(iota((32, NFFT), 0), 2)
    turns = jnp.zeros((32, NFFT), jnp.int32)
    for f in range(16):
        turns = jnp.where(freq == f, bins[f], turns)
    angle = (2.0 * math.pi) * lax.rem(turns * step, NFFT).astype(F32) / NFFT
    taper = (1.0 - jnp.cos((2.0 * math.pi) * step.astype(F32) / NFFT)) / math.sqrt(1.5 * NFFT)
    real = lax.rem(iota((32, NFFT), 0), 2) == 0
    window = (taper * jnp.where(real, jnp.cos(angle), -jnp.sin(angle))).astype(BF16)
    tile = (lax.rem(iota((NFFT, 512), 1), NFFT) == iota((NFFT, 512), 0)).astype(BF16)
    tiled = dot(window, tile).astype(BF16)
    spread = (lax.div(iota((256, 32), 0), 8) == iota((256, 32), 1)).astype(BF16)
    full = dot(spread, tiled)
    same = lax.rem(iota((256, 512), 0), 8) == lax.div(iota((256, 512), 1), NFFT)
    amat[...] = jnp.where(same, full, 0.0).astype(BF16)
    slot = iota((NFFT, 384), 1)
    when = jnp.where(slot < 264, slot, jnp.where(slot < 304, slot - 8, slot - 376))
    known = (slot < 264) | ((slot >= 272) & (slot < 304)) | ((slot >= 304) & (slot < 376))
    when = jnp.where(known, when, -100000) - iota((NFFT, 384), 0)
    for g in range(8):
        parts = []
        for b in range(8):
            begin = starts[8 * g + b] - 264 * g
            parts.append(jnp.where(when == begin, 1.0, 0.0).astype(BF16))
        pick = jnp.concatenate(parts, axis=0)
        mmat[g] = dot(amat[...], pick).astype(BF16)


def first_kernel(
    total_rows,     strain, starts, bins, zout, out,
    came, slab, amat, mmat, spec, zbuf, gram, packed, rc, sum4, rx, pz, rz, piece, ry, fin, gz, held,
    a_send, a_recv, own_sem, c_send, c_recv, x_send, x_recv, z_send, z_recv,
    y_send, y_recv, w_send, w_recv, f_send, f_recv, m_send, m_recv, out_sem, keep_sem,
):
    s, t, x, z, ylo, core, yhi = place()
    yy = yhi * 2 + ylo
    def tm_peer(dy, dc):
        return lax.rem(yhi + dy, 4) * 2 + lax.rem(core + dc, 2)

    tm_peers = [(s, tm_peer(*o)) for o in FAR_T]
    x_peers = {o: (space_of(lax.rem(x + o, NX), z, ylo), t) for o in FAR_4}
    z_peers = {o: (space_of(lax.rem(x + 8 - o, NX), lax.rem(z + o, NZ), ylo), t) for o in FAR_8}
    line = {o: (space_of(x, lax.rem(z + o, NZ), ylo), t) for o in (1, 2, 6, 7)}
    own = lax.rem(x + z, NX)

    def y_peer(o):
        other = lax.rem(yy + o, NY)
        return (space_of(x, z, lax.rem(other, 2)), lax.div(other, 2) * 2 + core)

    y_peers = {o: y_peer(o) for o in FAR_8}
    mate = (s, t + 1 - 2 * core)

    barrier = pltpu.get_barrier_semaphore()
    odd = {o: y_peers[o] for o in (1, 3, 5, 7)}
    greeted = tm_peers + list(x_peers.values()) + list(z_peers.values()) + list(odd.values()) + list(line.values())
    for peer in greeted:
        pl.semaphore_signal(barrier, inc=1, device_id=peer, device_id_type=MESH)
    pl.semaphore_wait(barrier, len(greeted))

    sends = []
    for c in range(3):
        for o in FAR_T:
            to = tm_peer(*o)
            n = o[0] * 2 + o[1]
            copy = remote(
                strain.at[c, :, pl.ds(pl.multiple_of(to * 128, 128), 128)],
                came.at[t, c], a_send.at[n, c], a_recv.at[n, c], (s, to),
            )
            copy.start()
            sends.append(copy)
    stay = pltpu.make_async_copy(
        strain.at[:, :, pl.ds(pl.multiple_of(t * 128, 128), 128)], came.at[t], own_sem
    )
    stay.start()

    build_windows(starts, bins, amat, mmat)
    slab[...] = jnp.zeros_like(slab)
    stay.wait()

    def square(c, f):
        rows = spec[pl.ds(2 * f, 2)].reshape(128, 128)
        high = rows.astype(BF16)
        low = (rows - high.astype(F32)).astype(BF16)
        both = jnp.concatenate([high, low], axis=0)
        zbuf[f, :, 128 * c : 128 * c + 128] = both
        quad = dot_t(both, both)
        return (quad[:128, :128] + quad[128:, 128:]) + (quad[:128, 128:] + quad[128:, :128])

    def product(c, f, carry):
        new = square(c, f)
        gram[f] = gram[f] + new if c else new
        return carry

    for c in range(3):
        for o in FAR_T:
            source = tm_peer(4 - o[0], o[1])
            n = o[0] * 2 + o[1]
            remote(
                came.at[source, c], came.at[source, c], a_send.at[n, c], a_recv.at[n, c], (s, source)
            ).wait_recv()
        for g in range(8):
            slab[g, 0:264, :] = came[g, c, :, :]
            if g < 7:
                slab[g, 272:304, :] = came[g + 1, c, 0:32, :]
            if g > 0:
                slab[g, 304:376, :] = came[g - 1, c, 192:264, :]
        for g in range(8):
            found = dot(mmat[g], slab[g])
            spec[:, 8 * g : 8 * g + 8, :] = found.reshape(32, 8, 128)

        if c < 2:
            lax.fori_loop(0, 16, functools.partial(product, c), 0)

    row, col = iota((128, 128), 0), iota((128, 128), 1)

    def finish(q):
        first = gram[2 * q] + square(2, 2 * q)
        second = gram[2 * q + 1] + square(2, 2 * q + 1)
        packed[q, 0:128, :] = jnp.where(row > col, first, second)
        diag = jnp.sum(jnp.where(row == col, first, 0.0), axis=0, keepdims=True)
        packed[q, 128:136, :] = jnp.broadcast_to(diag, (8, 128))

    there = {o: lax.rem(x + o, NX) for o in FAR_4 + (0,)}
    theirs = {o: (1 - core) * 4 + lax.rem(there[o] + z, NX) for o in there}
    ours = {o: core * 4 + lax.rem(there[o] + z, NX) for o in there}
    for o in there:
        finish(theirs[o])
    for o in there:
        copy = remote(packed.at[theirs[o]], rc.at[there[o]], c_send.at[o], c_recv.at[o], mate)
        copy.start()
        sends.append(copy)
    for o in there:
        if o in (2, 3):
            finish(ours[o])
            finish(ours[o - 1 if o == 2 else 0])
        xo, pair = there[o], ours[o]
        remote(packed.at[pair], rc.at[xo], c_send.at[o], c_recv.at[o], mate).wait_recv()
        if o:
            sum4[xo] = packed[pair] + rc[xo]
            copy = remote(sum4.at[xo], rx.at[x], x_send.at[o], x_recv.at[o], x_peers[o])
            copy.start()
            sends.append(copy)
        else:
            rx[x] = packed[pair] + rc[x]
    save = pltpu.make_async_copy(zbuf, zout, out_sem)
    save.start()
    for o in FAR_4:
        source = lax.rem(x + NX - o, NX)
        remote(sum4.at[source], rx.at[source], x_send.at[o], x_recv.at[o], x_peers[o]).wait_recv()
    mine = (rx[0] + rx[1]) + (rx[2] + rx[3])

    for i in range(NZ):
        pz[i, 0:16, :] = mine[16 * i : 16 * i + 16]
        pz[i, 16:24, :] = mine[128:136]
    for o in FAR_8:
        zo = lax.rem(z + o, NZ)
        copy = remote(pz.at[zo], rz.at[z], z_send.at[o], z_recv.at[o], z_peers[o])
        copy.start()
        sends.append(copy)
    rz[z] = pz[z]
    for o in FAR_8:
        source = lax.rem(z + NZ - o, NZ)
        remote(pz.at[source], rz.at[source], z_send.at[o], z_recv.at[o], z_peers[o]).wait_recv()
    piece[...] = ((rz[0] + rz[1]) + (rz[2] + rz[3])) + ((rz[4] + rz[5]) + (rz[6] + rz[7]))

    for o in FAR_8:
        copy = remote(piece, ry.at[yy], y_send.at[o], y_recv.at[o], y_peers[o])
        copy.start()
        sends.append(copy)
    ry[yy] = piece[...]
    for o in FAR_8:
        source = lax.rem(yy + NY - o, NY)
        remote(piece, ry.at[source], y_send.at[o], y_recv.at[o], y_peers[o]).wait_recv()
    fin[...] = ((ry[0] + ry[1]) + (ry[2] + ry[3])) + ((ry[4] + ry[5]) + (ry[6] + ry[7]))

    for o in FAR_8:
        copy = remote(fin.at[pl.ds(0, 16)], gz.at[z], w_send.at[o], w_recv.at[o], z_peers[o])
        copy.start()
        sends.append(copy)
    gz[z] = fin[0:16, :]
    for o in FAR_8:
        source = lax.rem(z + NZ - o, NZ)
        remote(fin.at[pl.ds(0, 16)], gz.at[source], w_send.at[o], w_recv.at[o], z_peers[o]).wait_recv()
    slot = core * 4 + own
    ways = []
    for band, (start, size) in enumerate(((0, 64), (64, 32), (96, 32))):
        rows = pl.ds(start, size)
        if band == 0:
            ways.append((band, 1, pl.ds(0, 32), line[2], 2))
            ways.append((band, 1, pl.ds(32, 32), line[6], 2))
        else:
            ways.append((band, 1, rows, line[2 if band == 1 else 6], 2))
        ways.append((band, 0, rows, x_peers[2], 2))
        ways.append((band, 0, rows, x_peers[1], 3))
        ways.append((band, 0, rows, x_peers[3], 1))
        ways.append((band, 1, rows, line[1], 3))
        ways.append((band, 1, rows, line[7], 1))
    bands = (pl.ds(0, 64), pl.ds(64, 32), pl.ds(96, 32))

    def final(band):
        for n, (which, k, rows, peer, _) in enumerate(ways):
            if which == band:
                part = held.at[slot, k, rows]
                copy = remote(part, part, f_send.at[n], f_recv.at[n], peer)
                copy.start()
                sends.append(copy)
        part = held.at[slot, :, bands[band]]
        copy = remote(part, part, m_send.at[20 + band], m_recv.at[20 + band], mate)
        copy.start()
        sends.append(copy)

    factor(total_rows, gz, fin, held, slot, final)

    order = [n for band in range(3) for d in (3, 1, 2) for n, w in enumerate(ways) if w[0] == band and w[4] == d]
    for n in order:
        _, k, rows, peer, back = ways[n]
        part = held.at[core * 4 + lax.rem(own + back, NX), k, rows]
        remote(part, part, f_send.at[n], f_recv.at[n], peer).wait_recv()
        copy = remote(part, part, m_send.at[n], m_recv.at[n], mate)
        copy.start()
        sends.append(copy)
    keep = [
        pltpu.make_async_copy(held.at[pl.ds(q * 4, 4)], out.at[pl.ds(q * 4, 4)], keep_sem.at[n])
        for n, q in enumerate((core, 1 - core))
    ]
    keep[0].start()
    for band in range(3):
        part = held.at[(1 - core) * 4 + own, :, bands[band]]
        remote(part, part, m_send.at[20 + band], m_recv.at[20 + band], mate).wait_recv()
    for n in order:
        _, k, rows, peer, back = ways[n]
        part = held.at[(1 - core) * 4 + lax.rem(own + back, NX), k, rows]
        remote(part, part, m_send.at[n], m_recv.at[n], mate).wait_recv()
    keep[1].start()

    for copy in sends:
        copy.wait_send()
    save.wait()
    for copy in keep:
        copy.wait()


def over_lanes(a, j):
    return jnp.broadcast_to(a[:, :, j : j + 1], a.shape)


def over_rows(a, i):
    return jnp.broadcast_to(a[:, i : i + 1, :], a.shape)


def factor(total_rows, g, fin, held, slot, final):
    lanes, subs = iota((1, 8, 128), 2), iota((1, 8, 128), 1)
    row, col = iota((128, 128), 0), iota((128, 128), 1)
    square = jnp.concatenate([g[i] for i in range(NZ)], axis=0) * (1.0 / total_rows)
    spare = fin[16:17, :] * (1.0 / total_rows)
    turned = square.T
    first = jnp.where(row == col, spare, jnp.where(row > col, square, turned))
    second = jnp.where(row > col, turned, square)
    m = [jnp.stack([first[8 * v : 8 * v + 8], second[8 * v : 8 * v + 8]]) for v in range(16)]
    for p in range(16):
        j0 = 8 * p
        top = m[p]
        here = (lanes >= j0) & (lanes < j0 + 8)
        columns = [over_lanes(top, j0 + k) for k in range(8)]
        a = [[over_rows(columns[k], i) for k in range(i + 1)] for i in range(8)]
        for k in range(8):
            r = lax.rsqrt(a[k][k])
            for q in range(k):
                a[k][q] = a[k][q] * r
            a[k][k] = r
            lower = {i: a[i][k] * r for i in range(k + 1, 8)}
            for i in range(k + 1, 8):
                for q in range(k):
                    a[i][q] = a[i][q] - lower[i] * a[k][q]
                a[i][k] = -(lower[i] * r)
                for q in range(k + 1, i + 1):
                    a[i][q] = a[i][q] - lower[i] * lower[q]

        def through(rows):
            done = []
            for i in range(8):
                total = a[i][0] * rows[0]
                for k in range(1, i + 1):
                    total = total + a[i][k] * rows[k]
                done.append(total)
            return done

        def joined(rows):
            whole = rows[7]
            for i in range(7):
                whole = jnp.where(subs == i, rows[i], whole)
            return whole

        base = jnp.where(here, jnp.where(lanes - j0 == subs, 1.0, 0.0), top)
        across = through([over_rows(base, k) for k in range(8)])
        corner = joined(through([over_rows(top, k) for k in range(8)]))
        held[slot, :, j0 : j0 + 8, :] = jnp.where(here & (lanes > j0 + subs), corner, joined(across))
        if p in (7, 11, 15):
            final((7, 11, 15).index(p))
        for v in range(p + 1, 16):
            left = through([over_lanes(m[v], j0 + k) for k in range(8)])
            rest = jnp.where(here, 0.0, m[v])
            for i in range(8):
                rest = rest - left[i] * across[i]
            m[v] = rest

def apply_kernel(pk, zz, upper, basis):
    row, col = iota((128, 128), 0), iota((128, 128), 1)
    step = pl.program_id(0)
    for k in range(8):
        both = pk[4 * step + k // 2, k % 2]
        upper[k] = jnp.where(col > row, both, jnp.where(col == row, 1.0 / both, 0.0))
        inverse = jnp.where(col <= row, both, 0.0)
        high = inverse.astype(BF16)
        low = (inverse - high.astype(F32)).astype(BF16)
        twice = jnp.concatenate([high, high], axis=1)
        found = dot(twice, zz[8 * step + k]) + dot(low, zz[8 * step + k, 0:128, :])
        for c in range(3):
            basis[k, c] = found[:, 128 * c : 128 * c + 128].astype(BF16)


def shards(strain, block_starts, bin_numbers):
    vmem = pl.BlockSpec(memory_space=pltpu.VMEM)
    smem = pl.BlockSpec(memory_space=pltpu.SMEM)
    hbm = pl.BlockSpec(memory_space=pl.ANY)
    dma = pltpu.SemaphoreType.DMA
    total_rows = 3.0 * 128 * lax.axis_size("space") * lax.axis_size("tm")
    zz, held = pl.pallas_call(
        functools.partial(first_kernel, total_rows),
        out_shape=(
            pltpu.VMEM((16, 256, 384), BF16),
            pltpu.VMEM((8, 2, 128, 128), F32),
        ),
        in_specs=[hbm, smem, smem],
        out_specs=(hbm, hbm),
        scratch_shapes=[
            pltpu.VMEM((NT, 3, 264, 128), BF16),
            pltpu.VMEM((8, 384, 128), BF16),
            pltpu.VMEM((256, 512), BF16),
            pltpu.VMEM((8, 256, 384), BF16),
            pltpu.VMEM((32, 64, 128), F32),
            pltpu.VMEM((16, 256, 384), BF16),
            pltpu.VMEM((16, 128, 128), F32),
            pltpu.VMEM((8, 136, 128), F32),
            pltpu.VMEM((4, 136, 128), F32),
            pltpu.VMEM((4, 136, 128), F32),
            pltpu.VMEM((4, 136, 128), F32),
            pltpu.VMEM((NZ, 24, 128), F32),
            pltpu.VMEM((NZ, 24, 128), F32),
            pltpu.VMEM((24, 128), F32),
            pltpu.VMEM((NY, 24, 128), F32),
            pltpu.VMEM((24, 128), F32),
            pltpu.VMEM((NZ, 16, 128), F32),
            pltpu.VMEM((8, 2, 128, 128), F32),
            dma((NT, 3)), dma((NT, 3)), dma,
            dma((4,)), dma((4,)), dma((4,)), dma((4,)),
            dma((8,)), dma((8,)), dma((8,)), dma((8,)), dma((8,)), dma((8,)),
            dma((20,)), dma((20,)), dma((23,)), dma((23,)), dma, dma((2,)),
        ],
        compiler_params=pltpu.CompilerParams(
            collective_id=0, has_side_effects=True, vmem_limit_bytes=58 * 1024 * 1024
        ),
    )(strain, block_starts, bin_numbers)
    upper, basis = pl.pallas_call(
        apply_kernel,
        grid=(2,),
        out_shape=(
            jax.ShapeDtypeStruct((16, 128, 128), F32),
            jax.ShapeDtypeStruct((16, 3, 128, 128), BF16),
        ),
        in_specs=[vmem, vmem],
        out_specs=(
            pl.BlockSpec((8, 128, 128), lambda i: (i, 0, 0)),
            pl.BlockSpec((8, 3, 128, 128), lambda i: (i, 0, 0, 0)),
        ),
        compiler_params=pltpu.CompilerParams(vmem_limit_bytes=24 * 1024 * 1024),
    )(held, zz)
    return upper, jnp.transpose(basis, (0, 2, 1, 3))


def solution(mesh):
    placed = (P(None, "tm", "space"), P(), P())
    return jax.shard_map(
        shards,
        mesh=mesh,
        in_specs=placed,
        out_specs=(P(), P(None, None, None, ("space", "tm"))),
        check_vma=False,
    )
```
